32 devices in a mesh: groups: 2 (over y), dom: 4 (over z), head: 2 (over x), aux: 2 (over core).
Axes of the slice: x: 2, y: 2, z: 4, core: 2. Of those that a mesh axis runs over, the one named last changes fastest.
Arguments:
- features: float32 [4096, 192], P(('groups', 'dom', 'aux')), parts along dimension 0, may hold values from -6 to 6
- face_weight: float32 [24576], P(('groups', 'dom', 'aux')), parts along dimension 0, may hold values from 0.5 to 2
- faces: int32 [3, 24576], P(None, ('groups', 'dom', 'aux')), parts along dimension 1, may hold values from 0 to 255, as said below
- face_live: int32 [16], P(('groups', 'dom', 'aux')), parts along dimension 0, may hold values from 24 to 1536, as said below
- send_index: int32 [2, 512], P(None, ('groups', 'dom', 'aux')), parts along dimension 1, may hold values from 0 to 255
- anchor_index: int32 [1024], P(('groups', 'dom', 'head', 'aux')), parts along dimension 0, may hold values from 0 to 255
- w_in: float32 [384, 768], P(None, 'head'), may hold values from -0.3125 to 0.3125
- w_out: float32 [768, 192], P('head'), may hold values from -0.21875 to 0.21875
- w_query: float32 [192, 192], replicated, may hold values from -8 to 8
- w_key: float32 [192, 192], replicated, may hold values from -8 to 8
- w_value: float32 [192, 192], replicated, may hold values from -0.4375 to 0.4375
- w_attn_out: float32 [192, 192], replicated, may hold values from -0.4375 to 0.4375
- out_grad: float32 [4096, 192], P(('groups', 'dom', 'aux')), parts along dimension 0, may hold values from -6 to 6
Outputs:
- output: float32 [4096, 192], P(('groups', 'dom', 'aux')), parts along dimension 0
- anchor_grad: float32 [1024, 192], P(('groups', 'dom', 'head', 'aux')), parts along dimension 0
The draws below stay inside these ranges and needn't reach their ends.
There are 2 independent parts, one for each index of `groups`. The reference program is written for one: setup_inputs(seed, part) draws one part's arguments, and reference() takes and returns one part's arrays. A program takes and returns all parts, laid end to end along the dimension named above; an argument that names none is the same for every part. Nothing has to cross between parts.
Inputs may be any that keep to these rules, and one draw needn't show every extreme that they name: `faces`: row 0 is a row of the receiving block; row 1 is 0 (own block), 1 (lower neighbour along dom) or 2 (upper); row 2 is a row of the own block when row 1 is 0, else a slot below 32 of that neighbour's halo rows. `face_live`: live face slots of a block come first; some block has all 1536 live.
All inputs are finite; a program needn't handle non-finite values.
Results may differ from the reference program's by a relative error of at most 0.0003.
Values sent between devices are 32-bit elements; how exact they have to be, the bound alone decides.
No kernel may reach another device: no remote copies, remote signals or barrier semaphores. Data moves between devices by JAX's collectives and lax.ppermute only.
A program may use at most 64 MiB of HBM per device.

```python
import math
import jax
import jax.numpy as jnp
from jax import lax

C = 192
HEADS = 3
F = 768
CELL_DEV = 256
ANC_DEV = 32
DH = 64
CAP = 32
FACE_DEV = 1536
SUBDOMAINS = 8
CELLS = 2048
FACES = 12288
HALOS = 256
ANCHORS = 512
N_DOM = 4
N_HEAD = 2
N_AUX = 2


def draw_faces(key, part):
    key = jax.random.fold_in(key, 1)
    first, second, third, fourth = jax.random.split(key, 4)
    receiver = jax.random.randint(first, (FACES,), 0, CELL_DEV)
    kind = jax.random.randint(second, (FACES,), 0, 10)
    source_part = jnp.where(kind == 8, 1, jnp.where(kind == 9, 2, 0))
    local_source = jax.random.randint(third, (FACES,), 0, CELL_DEV)
    halo_source = jax.random.randint(fourth, (FACES,), 0, CAP)
    source = jnp.where(source_part == 0, local_source, halo_source)
    return jnp.stack([receiver, source_part, source]).astype(jnp.int32)


def draw_face_live(key, part):
    key = jax.random.fold_in(key, 2)
    first, second = jax.random.split(key, 2)
    level = jax.random.randint(first, (SUBDOMAINS,), 0, 8)
    counts = FACE_DEV // 64 * (1 + level * level)
    fullest = jax.random.randint(second, (), 0, SUBDOMAINS)
    counts = jnp.where(jnp.arange(SUBDOMAINS) == fullest, FACE_DEV, counts)
    return counts.astype(jnp.int32)


def wave_direction():
    index = lax.broadcasted_iota(jnp.float32, (C,), 0)
    return math.sqrt(2.0 / C) * jnp.cos(2.0 * math.pi * 5.0 * (index + 0.5) / C)


def common_part(key):
    column_factor = jax.random.normal(jax.random.fold_in(key, 11), (C,), jnp.float32)
    strength = math.sqrt(300.0 / C / math.sqrt(DH))
    return strength * wave_direction()[:, None] * column_factor[None, :]


def draw_features(key, part):
    key = jax.random.fold_in(key, 5)
    first = jax.random.fold_in(key, 0)
    result = jax.random.normal(first, (CELLS, C), jnp.float32)
    return jnp.clip(result, -6.0, 6.0)


def draw_w_query(key, part):
    base = key
    key = jax.random.fold_in(key, 3)
    own = jax.random.normal(key, (C, C), jnp.float32)
    result = common_part(base) + own * (1.0 / math.sqrt(C))
    return jnp.clip(result, -8.0, 8.0)


def draw_w_key(key, part):
    base = key
    key = jax.random.fold_in(key, 4)
    own = jax.random.normal(key, (C, C), jnp.float32)
    result = common_part(base) + own * (1.0 / math.sqrt(C))
    return jnp.clip(result, -8.0, 8.0)


def touch_ends(values, rng, low, largest):
    shape = values.shape
    spot = [jax.random.randint(jax.random.fold_in(rng, axis), (), 0, shape[axis]) for axis in range(len(shape))]
    values = values.at[tuple(spot)].set(low)
    longest = shape.index(max(shape))
    spot[longest] = (spot[longest] + 1) % shape[longest]
    return values.at[tuple(spot)].set(largest)


def block_scale(rng, dims, cuts, smallest, largest):
    factor_of, own = 1.0, jax.random.fold_in(rng, 6)
    for axis_at, blocks in cuts:
        heights = jnp.exp(jax.random.uniform(jax.random.fold_in(own, axis_at), (blocks,), jnp.float32, smallest / len(cuts), largest / len(cuts)))
        factor_of = factor_of * jnp.repeat(heights, dims[axis_at] // blocks).reshape([-1 if axis == axis_at else 1 for axis in range(len(dims))])
    return factor_of


def scatter_about(key, dims, deviation, limit, cuts=(), kind=jnp.bfloat16):
    drawn = jax.random.normal(key, dims, jnp.float32) * deviation
    if len(cuts) > 0:
        drawn = block_scale(key, dims, cuts, -0.22, 0.18) * drawn
    return jnp.clip(drawn, min=-limit, max=limit).astype(kind)


def setup_inputs(seed: int = 0, part: int = 0) -> dict:
    key_list = jax.random.split(jax.random.key(seed), 14)
    own_keys = jax.random.split(jax.random.fold_in(key_list[13], part), 14)
    features = draw_features(jax.random.fold_in(jax.random.fold_in(key_list[13], part), 71), part)
    face_weight = jnp.clip(jnp.exp(math.log(2.0) - 1.3862944 * jax.random.uniform(own_keys[1], (FACES,), jnp.float32) ** block_scale(own_keys[1], (FACES,), ((0, 8),), -0.2, 0.2)), 0.5, 2.0)
    faces = draw_faces(jax.random.fold_in(jax.random.fold_in(key_list[13], part), 71), part)
    face_live = draw_face_live(jax.random.fold_in(jax.random.fold_in(key_list[13], part), 71), part)
    send_index = touch_ends(jax.random.randint(own_keys[4], (2, HALOS), 0, CELL_DEV), jax.random.fold_in(own_keys[4], 1), 0, CELL_DEV - 1).astype(jnp.int32)
    anchor_index = touch_ends(jax.random.randint(own_keys[5], (ANCHORS,), 0, CELL_DEV), jax.random.fold_in(own_keys[5], 1), 0, CELL_DEV - 1).astype(jnp.int32)
    w_in = scatter_about(key_list[6], (2 * C, F), (2 * C) ** -0.5, 0.3125, ((1, 2),), jnp.float32)
    w_out = scatter_about(key_list[7], (F, C), F ** -0.5, 0.21875, ((0, 2),), jnp.float32)
    w_query = draw_w_query(jax.random.fold_in(key_list[13], 71), part)
    w_key = draw_w_key(jax.random.fold_in(key_list[13], 71), part)
    w_value = scatter_about(key_list[10], (C, C), C ** -0.5, 0.4375, (), jnp.float32)
    w_attn_out = scatter_about(key_list[11], (C, C), C ** -0.5, 0.4375, (), jnp.float32)
    out_grad = scatter_about(own_keys[12], (CELLS, C), 1.0, 6.0, ((0, 8),), jnp.float32)
    return dict(features=features, face_weight=face_weight, faces=faces, face_live=face_live, send_index=send_index, anchor_index=anchor_index, w_in=w_in, w_out=w_out, w_query=w_query, w_key=w_key, w_value=w_value, w_attn_out=w_attn_out, out_grad=out_grad)


HIGH = lax.Precision.HIGHEST

def matmul(left, right):
    return jnp.dot(left, right, precision=HIGH, preferred_element_type=jnp.float32)

def layer_norm(value):
    mean = lax.optimization_barrier(jnp.mean(value, axis=-1, keepdims=True))
    centred = value - mean
    spread = lax.optimization_barrier(jnp.mean(centred * centred, axis=-1, keepdims=True))
    return centred * lax.rsqrt(spread + 1e-05)

def reference(features, face_weight, faces, face_live, send_index, anchor_index, w_in, w_out, w_query, w_key, w_value, w_attn_out, out_grad):
    subs = N_DOM * N_AUX
    normed = layer_norm(features)
    blocks = normed.reshape(N_DOM, N_AUX, CELL_DEV, C)
    sends = send_index.reshape(2, N_DOM, N_AUX, CAP)
    to_lower = jnp.take_along_axis(blocks, sends[0][..., None], axis=2)
    to_upper = jnp.take_along_axis(blocks, sends[1][..., None], axis=2)
    from_lower = jnp.roll(to_upper, 1, axis=0)
    from_upper = jnp.roll(to_lower, -1, axis=0)
    extended = jnp.concatenate([blocks, from_lower, from_upper], axis=2).reshape(subs, CELL_DEV + 2 * CAP, C)
    face_rows = faces.reshape(3, subs, FACE_DEV)
    weights = face_weight.reshape(subs, FACE_DEV)
    live = jnp.arange(FACE_DEV, dtype=jnp.int32)[None, :] < face_live[:, None]
    weights = jnp.where(live, weights, jnp.zeros_like(weights))
    offset = jnp.where(face_rows[1] == 0, 0, jnp.where(face_rows[1] == 1, CELL_DEV, CELL_DEV + CAP)).astype(jnp.int32)
    source = (face_rows[2] + offset).astype(jnp.int32)
    messages = jnp.take_along_axis(extended, source[..., None], axis=1) * weights[..., None]
    agg = jax.vmap(lambda msg, dest: jax.ops.segment_sum(msg, dest, num_segments=CELL_DEV))(messages, face_rows[0])
    agg = agg.reshape(CELLS, C)
    hidden = jax.nn.gelu(matmul(jnp.concatenate([normed, agg], axis=1), w_in), approximate=False)
    mixed = features + matmul(hidden, w_out)
    query_normed = layer_norm(mixed)
    query = matmul(query_normed, w_query)
    anchors = anchor_index.reshape(N_DOM, N_HEAD, N_AUX, ANC_DEV)
    dom_ids = lax.broadcasted_iota(jnp.int32, anchors.shape, 0)
    aux_ids = lax.broadcasted_iota(jnp.int32, anchors.shape, 2)
    rows = ((dom_ids * N_AUX + aux_ids) * CELL_DEV + anchors).reshape(ANCHORS).astype(jnp.int32)
    anchor_feats = query_normed[rows]
    keys = matmul(anchor_feats, w_key)
    values = matmul(anchor_feats, w_value)
    d_att = matmul(out_grad, w_attn_out.T)
    scale = 1.0 / math.sqrt(DH)

    def block_step(carry, pieces):
        q_block, g_block = pieces
        grad_k, grad_v = carry
        outs, keys_parts, value_parts = ([], [], [])
        for head in range(HEADS):
            cols = slice(head * DH, (head + 1) * DH)
            q_head = q_block[:, cols]
            g_head = g_block[:, cols]
            v_head = values[:, cols]
            scores = matmul(q_head, keys[:, cols].T) * scale
            top = lax.optimization_barrier(jnp.max(scores, axis=1, keepdims=True))
            expo = jnp.exp(scores - top)
            probs = expo / lax.optimization_barrier(jnp.sum(expo, axis=1, keepdims=True))
            att = matmul(probs, v_head)
            dprob = matmul(g_head, v_head.T)
            delta = lax.optimization_barrier(jnp.sum(g_head * att, axis=1, keepdims=True))
            dscore = probs * (dprob - delta)
            keys_parts.append(matmul(dscore.T, q_head) * scale)
            value_parts.append(matmul(probs.T, g_head))
            outs.append(att)
        grad_k = grad_k + jnp.concatenate(keys_parts, axis=1)
        grad_v = grad_v + jnp.concatenate(value_parts, axis=1)
        return ((grad_k, grad_v), jnp.concatenate(outs, axis=1))
    zeros = jnp.zeros((ANCHORS, C), jnp.float32)
    (grad_k, grad_v), attended = lax.scan(block_step, (zeros, zeros), (query.reshape(subs, CELL_DEV, C), d_att.reshape(subs, CELL_DEV, C)))
    output = mixed + matmul(attended.reshape(CELLS, C), w_attn_out)
    anchor_grad = matmul(grad_k, w_key.T) + matmul(grad_v, w_value.T)
    return (output, anchor_grad)
```

```python
import functools
import math

import jax
import jax.numpy as jnp
from jax import lax
from jax.experimental import pallas as pl
from jax.experimental.pallas import tpu as pltpu
from jax.sharding import PartitionSpec as P

HEADS = 3
DH = 64
HIGH = lax.Precision.HIGH
NN = (((1,), (0,)), ((), ()))
NT = (((1,), (1,)), ((), ()))
BF = jnp.bfloat16
F32 = jnp.float32


def dot(left, right, dims=NN, precision=HIGH):
    return lax.dot_general(left, right, dims, precision=precision, preferred_element_type=F32)


def dot_bf(left, right, dims=NN):
    return lax.dot_general(left, right, dims, preferred_element_type=F32)


def split(value):
    top = value.astype(BF)
    return top, (value - top.astype(F32)).astype(BF)


def layer_norm(value):
    mean = jnp.mean(value, axis=-1, keepdims=True)
    centred = value - mean
    spread = jnp.mean(centred * centred, axis=-1, keepdims=True)
    return centred * lax.rsqrt(spread + 1e-05)


def call(body, outs, ins, smem=(), scratch=(), flops=10**8):
    specs = [
        pl.BlockSpec(memory_space=pltpu.SMEM if i in smem else pltpu.VMEM)
        for i in range(len(ins))
    ]
    return pl.pallas_call(
        body,
        out_shape=[jax.ShapeDtypeStruct(s, F32) for s in outs],
        in_specs=specs,
        out_specs=[pl.BlockSpec(memory_space=pltpu.VMEM)] * len(outs),
        scratch_shapes=list(scratch),
        compiler_params=pltpu.CompilerParams(vmem_limit_bytes=48 * 2**20),
        cost_estimate=pl.CostEstimate(flops=flops, bytes_accessed=10**6, transcendentals=0),
    )(*ins)


def take_rows(source, index, count, target):
    if count <= 64:
        for i in range(count):
            target[pl.ds(i, 1), :] = source[pl.ds(index(i), 1), :]
    else:

        def step(i, carry):
            target[pl.ds(i, 1), :] = source[pl.ds(index(i), 1), :]
            return carry

        lax.fori_loop(0, count, step, 0)


def take_anchors(head_ref, own_ref, other_ref, source, target):
    own = own_ref.shape[1]
    n_head = other_ref.shape[1] // own + 1
    for place in range(n_head):
        step = lax.rem(head_ref[0] - place + n_head, n_head)
        base = jnp.maximum(step - 1, 0) * own

        def index(i, step=step, base=base):
            return jnp.where(step == 0, own_ref[0, i], other_ref[0, base + i])

        take_rows(source, index, own, target.at[pl.ds(place * own, own)])


def outgoing_kernel(parity_ref, send_ref, x_ref, first_ref, second_ref):
    parity = parity_ref[0]
    count = first_ref.shape[0]
    take_rows(x_ref, lambda i: send_ref[1 - parity, i], count, first_ref)
    take_rows(x_ref, lambda i: send_ref[parity, i], count, second_ref)
    first_ref[...] = layer_norm(first_ref[...])
    second_ref[...] = layer_norm(second_ref[...])


def own_faces_kernel(
    parity_ref, live_ref, head_ref, own_ref, other_ref, x_ref, faces_ref, weight_ref, w_in_ref,
    pre_ref, halo_mat_ref, anchor_ref,
):
    rows, width = x_ref.shape
    halos = halo_mat_ref.shape[1] // 2
    slots = faces_ref.shape[1]
    x = x_ref[...]
    normed = layer_norm(x)
    take_anchors(head_ref, own_ref, other_ref, x_ref, anchor_ref)
    receiver = faces_ref[0:1, :]
    kind = faces_ref[1:2, :]
    first_kind = 2 - parity_ref[0]
    offset = jnp.where(kind == 0, 0, jnp.where(kind == first_kind, rows, rows + halos))
    source = faces_ref[2:3, :] + offset
    live = lax.broadcasted_iota(jnp.int32, (1, slots), 1) < live_ref[0]
    weight = jnp.where(live, weight_ref[...], 0.0)
    top = weight.astype(BF).astype(F32)
    low = (weight - top).astype(BF).astype(F32)
    into = jnp.where(
        lax.broadcasted_iota(jnp.int32, (rows, slots), 0) == receiver, 1.0, 0.0
    ).astype(BF)
    match = lax.broadcasted_iota(jnp.int32, (rows + 2 * halos, slots), 0) == source
    matrix = dot_bf(into, jnp.where(match, top, 0.0).astype(BF), NT)
    matrix = matrix + dot_bf(into, jnp.where(match, low, 0.0).astype(BF), NT)
    halo_mat_ref[...] = matrix[:, rows:]
    agg = dot(matrix[:, :rows], normed)
    pre_ref[...] = dot(normed, w_in_ref[:width]) + dot(agg, w_in_ref[width:])


def mlp_kernel(
    head_ref, own_ref, other_ref, first_ref, second_ref, pre_ref, halo_mat_ref, w_in_ref, w_out_ref,
    part_ref, anchor_ref,
):
    width = first_ref.shape[1]
    halo = jnp.concatenate([first_ref[...], second_ref[...]], axis=0)
    halo = dot(halo, w_in_ref[width:])
    pre = pre_ref[...] + dot(halo_mat_ref[...], halo)
    hidden = 0.5 * pre * (1.0 + lax.erf(pre * math.sqrt(0.5)))
    part_ref[...] = dot(hidden, w_out_ref[...])
    take_anchors(head_ref, own_ref, other_ref, part_ref, anchor_ref)


def grad_in_kernel(g_ref, w_ref, d_ref, d_t_ref):
    d = dot(g_ref[...], w_ref[...], NT)
    d_ref[...] = d
    d_t_ref[...] = d.T


def anchor_kernel(x_ref, part_ref, recv_ref, out_ref):
    out_ref[...] = layer_norm(x_ref[...] + (part_ref[...] + recv_ref[...]))


def query_kernel(x_ref, part_ref, recv_ref, w_ref, mixed_ref, q_ref, q_t_ref):
    mixed = x_ref[...] + (part_ref[...] + recv_ref[...])
    mixed_ref[...] = mixed
    q = dot(layer_norm(mixed), w_ref[...]) * (1.0 / math.sqrt(DH))
    q_ref[...] = q
    q_t_ref[...] = q.T


def pairs(value):
    top, low = split(value)
    return jnp.concatenate([top, low, top, low], axis=1)


def pairs_right(value):
    top, low = split(value)
    return jnp.concatenate([top, top, low, low], axis=1)


def wide(value):
    top, low = split(value)
    return jnp.concatenate([top, low], axis=1)


def attention_kernel(blocks, own, head_ref, *refs):
    feats = refs[:blocks]
    q_ref, q_t_ref, d_ref, d_t_ref, wk_ref, wv_ref, att_ref, keep_ref, give_ref = refs[
        blocks : blocks + 9
    ]
    n_head = feats[0].shape[0] // own
    head = head_ref[0]

    def of_head(step):
        start = pl.multiple_of(lax.rem(head + step, n_head) * own, own)
        return jnp.concatenate([f[pl.ds(start, own), :] for f in feats], axis=0)

    mine = of_head(0)
    rest = jnp.concatenate([of_head(step) for step in range(1, n_head)], axis=0)
    count = mine.shape[0]
    rest_count = rest.shape[0]
    chunk = min(rest_count, 512)
    wk, wv = wk_ref[...], wv_ref[...]
    k_mine, v_mine = dot(mine, wk), dot(mine, wv)
    if rest_count == chunk:
        k_rest, v_rest = dot(rest, wk), dot(rest, wv)
    else:
        rest_ref = refs[-1]
        rest_ref[...] = rest
    grads_k, grads_v = [], []
    for at in range(HEADS):
        cols = slice(at * DH, (at + 1) * DH)
        q_pairs = pairs(q_ref[:, cols])
        d = d_ref[:, cols]
        score = dot_bf(q_pairs, pairs_right(k_mine[:, cols]), NT)
        v_wide = wide(v_mine[:, cols])
        if rest_count == chunk:
            score_rest = dot_bf(q_pairs, pairs_right(k_rest[:, cols]), NT)
            top = jnp.maximum(
                jnp.max(score, axis=1, keepdims=True), jnp.max(score_rest, axis=1, keepdims=True)
            )
            expo = jnp.exp(score - top)
            expo_rest = jnp.exp(score_rest - top)
            total = jnp.sum(expo, axis=1, keepdims=True) + jnp.sum(
                expo_rest, axis=1, keepdims=True
            )
            e_top, e_low = split(expo_rest)
            rest_wide = wide(v_rest[:, cols])
            acc = dot_bf(e_top, rest_wide) + dot_bf(e_low, rest_wide)
        else:
            top = jnp.max(score, axis=1, keepdims=True)

            def step(i, state):
                top, total, acc = state
                feat = rest_ref[pl.ds(pl.multiple_of(i * chunk, chunk), chunk), :]
                score_rest = dot_bf(q_pairs, pairs_right(dot(feat, wk_ref[:, cols])), NT)
                new = jnp.maximum(top, jnp.max(score_rest, axis=1, keepdims=True))
                expo_rest = jnp.exp(score_rest - new)
                factor = jnp.exp(top - new)
                total = total * factor + jnp.sum(expo_rest, axis=1, keepdims=True)
                e_top, e_low = split(expo_rest)
                rest_wide = wide(dot(feat, wv_ref[:, cols]))
                acc = acc * factor + dot_bf(e_top, rest_wide) + dot_bf(e_low, rest_wide)
                return new, total, acc

            start = (top, jnp.zeros_like(top), jnp.zeros((q_ref.shape[0], 2 * DH), F32))
            top, total, acc = lax.fori_loop(0, rest_count // chunk, step, start)
            expo = jnp.exp(score - top)
            total = total + jnp.sum(expo, axis=1, keepdims=True)
        e_top, e_low = split(expo)
        acc = acc + (dot_bf(e_top, v_wide) + dot_bf(e_low, v_wide))
        inverse = 1.0 / total
        att = (acc[:, :DH] + acc[:, DH:]) * inverse
        att_ref[:, cols] = att
        probs = expo * inverse
        d_prob = dot_bf(pairs(d), pairs_right(v_mine[:, cols]), NT)
        delta = jnp.sum(d * att, axis=1, keepdims=True)
        s_top, s_low = split(probs * (d_prob - delta))
        p_top, p_low = split(probs)
        q_t = jnp.concatenate(split(q_t_ref[cols, :]), axis=0)
        d_t = jnp.concatenate(split(d_t_ref[cols, :]), axis=0)
        grad_k = dot_bf(q_t, s_top) + dot_bf(q_t, s_low)
        grad_v = dot_bf(d_t, p_top) + dot_bf(d_t, p_low)
        grads_k.append(grad_k[:DH] + grad_k[DH:])
        grads_v.append(grad_v[:DH] + grad_v[DH:])
    grad_k = jnp.concatenate(grads_k, axis=0)
    grad_v = jnp.concatenate(grads_v, axis=0)
    grad = (dot(wk, grad_k) + dot(wv, grad_v)).T
    keep_ref[...] = grad[: count // 2]
    give_ref[...] = grad[count // 2 :]


def add_kernel(own, keep_ref, recv_ref, *outs):
    for i, out in enumerate(outs):
        rows = pl.ds(i * own, own)
        out[...] = keep_ref[rows, :] + recv_ref[rows, :]


def output_kernel(mixed_ref, att_ref, w_ref, out_ref):
    out_ref[...] = mixed_ref[...] + dot(att_ref[...], w_ref[...])


def sum_kernel(*refs):
    total = refs[0][...]
    for ref in refs[1:-1]:
        total = total + ref[...]
    refs[-1][...] = total


def shards(
    features,
    face_weight,
    faces,
    face_live,
    send_index,
    anchor_index,
    w_in,
    w_out,
    w_query,
    w_key,
    w_value,
    w_attn_out,
    out_grad,
):
    rows, width = features.shape
    halos = send_index.shape[1]
    units = w_in.shape[1]
    own = anchor_index.shape[0]
    n_dom, n_head, n_aux = (lax.axis_size(a) for a in ("dom", "head", "aux"))
    assert n_dom % 2 == 0 and n_aux == 2
    anchors = own * n_head
    head = lax.axis_index("head").astype(jnp.int32).reshape(1)
    parity = (lax.axis_index("dom") % 2).astype(jnp.int32).reshape(1)
    swap = [(0, 1), (1, 0)]
    inner = [(i, i ^ 1) for i in range(n_dom)]
    outer = [(i, (i - 1 if i % 2 == 0 else i + 1) % n_dom) for i in range(n_dom)]

    def across(value, step):
        if n_dom & (n_dom - 1) == 0:
            perm = [(i, i ^ step) for i in range(n_dom)]
        else:
            perm = [(i, (i + step) % n_dom) for i in range(n_dom)]
        return lax.ppermute(value, "dom", perm)

    def back(step):
        return step if n_dom & (n_dom - 1) == 0 else n_dom - step

    index = anchor_index.reshape(1, own)
    other_index = [
        lax.ppermute(index, "head", [(i, (i + s) % n_head) for i in range(n_head)])
        for s in range(1, n_head)
    ]
    other_index = other_index[0] if n_head == 2 else jnp.concatenate(other_index, axis=1)

    def head_sum(part):
        if n_head == 2:
            return part, lax.ppermute(part, "head", swap)
        return lax.psum(part, "head"), jnp.zeros_like(part)

    first, second = call(
        outgoing_kernel, [(halos, width)] * 2, [parity, send_index, features], smem=(0, 1)
    )
    first = lax.ppermute(first, "dom", inner)
    second = lax.ppermute(second, "dom", outer)
    pre, halo_mat, anchor_x = call(
        own_faces_kernel,
        [(rows, units), (rows, 2 * halos), (anchors, width)],
        [
            parity, face_live, head, index, other_index,
            features, faces, face_weight.reshape(1, -1), w_in,
        ],
        smem=(0, 1, 2, 3, 4),
        flops=2 * 10**9,
    )
    part, anchor_part = call(
        mlp_kernel,
        [(rows, width), (anchors, width)],
        [head, index, other_index, first, second, pre, halo_mat, w_in, w_out],
        smem=(0, 1, 2),
        flops=10**9,
    )
    anchor_part, anchor_recv = head_sum(anchor_part)
    part, recv = head_sum(part)
    d, d_t = call(grad_in_kernel, [(rows, width), (width, rows)], [out_grad, w_attn_out])
    (feat,) = call(anchor_kernel, [(anchors, width)], [anchor_x, anchor_part, anchor_recv])
    feats = [feat] + [across(feat, s) for s in range(1, n_dom)]
    mixed, q, q_t = call(
        query_kernel,
        [(rows, width), (rows, width), (width, rows)],
        [features, part, recv, w_query],
        flops=10**9,
    )
    feats = feats + [lax.ppermute(f, "aux", swap) for f in feats]
    half = n_dom * own
    att, keep, give = call(
        functools.partial(attention_kernel, len(feats), own),
        [(rows, width), (half, width), (half, width)],
        [head, *feats, q, q_t, d, d_t, w_key, w_value],
        smem=(0,),
        scratch=[pltpu.VMEM((half * 2 * (n_head - 1), width), F32)] if n_head > 2 else [],
        flops=2 * 10**9,
    )
    recv = lax.ppermute(give, "aux", swap)
    sums = call(functools.partial(add_kernel, own), [(own, width)] * n_dom, [keep, recv])
    sums = [sums[0]] + [across(sums[s], back(s)) for s in range(1, n_dom)]
    (output,) = call(output_kernel, [(rows, width)], [mixed, att, w_attn_out])
    (anchor_grad,) = call(sum_kernel, [(own, width)], sums)
    return output, anchor_grad


def solution(mesh):
    placed = (
        P(("groups", "dom", "aux"), None),
        P(("groups", "dom", "aux")),
        P(None, ("groups", "dom", "aux")),
        P(("groups", "dom", "aux")),
        P(None, ("groups", "dom", "aux")),
        P(("groups", "dom", "head", "aux")),
        P(None, "head"),
        P("head", None),
        P(),
        P(),
        P(),
        P(),
        P(("groups", "dom", "aux"), None),
    )
    return jax.shard_map(
        shards,
        mesh=mesh,
        in_specs=placed,
        out_specs=(P(("groups", "dom", "aux"), None), P(("groups", "dom", "head", "aux"), None)),
        check_vma=False,
    )
```

```python
import functools
import math

import jax
import jax.numpy as jnp
from jax import lax
from jax.experimental import pallas as pl
from jax.experimental.pallas import tpu as pltpu
from jax.sharding import PartitionSpec as P

HEADS = 3
DH = 64
NN = (((1,), (0,)), ((), ()))
NT = (((1,), (1,)), ((), ()))
TN = (((0,), (0,)), ((), ()))
BF = jnp.bfloat16
F32 = jnp.float32
I32 = jnp.int32
LOG2E = math.log2(math.e)


def dot_bf(left, right, dims=NN):
    return lax.dot_general(left, right, dims, preferred_element_type=F32)


def split(value):
    top = value.astype(BF)
    return top, (value - top.astype(F32)).astype(BF)


def dot_halves(left, right, dims=NN):
    rows = left[0].shape[0]
    both = dot_bf(jnp.concatenate(left, axis=0), right[0], dims)
    return both[:rows] + (both[rows:] + dot_bf(left[0], right[1], dims))


def dot(left, right, dims=NN):
    return dot_halves(split(left), split(right), dims)


def layer_norm(value, axis=-1):
    mean = jnp.mean(value, axis=axis, keepdims=True)
    centred = value - mean
    spread = jnp.mean(centred * centred, axis=axis, keepdims=True)
    return centred * lax.rsqrt(spread + 1e-05)


def call(body, outs, ins, smem=(), hbm=(), scratch=(), flops=10**8):
    def space(i):
        return pltpu.SMEM if i in smem else pltpu.HBM if i in hbm else pltpu.VMEM

    return pl.pallas_call(
        body,
        out_shape=[jax.ShapeDtypeStruct(o[:2], o[2] if len(o) > 2 else F32) for o in outs],
        in_specs=[pl.BlockSpec(memory_space=space(i)) for i in range(len(ins))],
        out_specs=[pl.BlockSpec(memory_space=pltpu.VMEM)] * len(outs),
        scratch_shapes=list(scratch),
        compiler_params=pltpu.CompilerParams(vmem_limit_bytes=48 * 2**20),
        cost_estimate=pl.CostEstimate(flops=flops, bytes_accessed=10**6, transcendentals=0),
    )(*[
        pltpu.with_memory_space_constraint(x, pltpu.HBM) if i in hbm else x
        for i, x in enumerate(ins)
    ])


def chosen(index, rows):
    places = lax.broadcasted_iota(I32, (rows, index.shape[1]), 0)
    return jnp.where(places == index, 1.0, 0.0).astype(BF)


def exact_parts(value):
    top, mid = split(value)
    return top, mid, (value - top.astype(F32) - mid.astype(F32)).astype(BF)


def outgoing_kernel(
    send_hbm, index_hbm, faces_hbm, x_t_hbm, w_in_hbm,
    lower_ref, upper_ref, index_ref, faces_ref, x_t_ref, w_in_ref, send_ref, sems,
):
    copies = [
        pltpu.make_async_copy(source, target, sems.at[i])
        for i, (source, target) in enumerate(
            [
                (send_hbm, send_ref), (x_t_hbm, x_t_ref), (index_hbm, index_ref),
                (faces_hbm, faces_ref), (w_in_hbm, w_in_ref),
            ]
        )
    ]
    for copy in copies:
        copy.start()
    copies[0].wait()
    halos = lower_ref.shape[0]
    index = jnp.concatenate([send_ref[0:1, :], send_ref[1:2, :]], axis=1)
    pick = chosen(index, x_t_ref.shape[1])
    copies[1].wait()
    top, mid, low = exact_parts(x_t_ref[...])
    sent = layer_norm((dot_bf(top, pick) + dot_bf(mid, pick) + dot_bf(low, pick)).T)
    lower_ref[...] = sent[:halos]
    upper_ref[...] = sent[halos:]
    for copy in copies[2:]:
        copy.wait()


def small_chosen(index, rows, value):
    places = lax.broadcasted_iota(I32, (rows, index.shape[1]), 0).astype(F32).astype(BF)
    return jnp.where(places == index, value, jnp.zeros_like(value))


def own_faces_kernel(
    live_ref, x_t_ref, faces_ref, weight_ref, w_in_ref,
    pre_t_ref, halo_mat_ref, w_top_ref, w_low_ref,
):
    width, rows = x_t_ref.shape
    units = pre_t_ref.shape[0]
    halos = halo_mat_ref.shape[0] // 2
    slots = faces_ref.shape[1]
    w_top, w_low = split(
        jnp.concatenate([w_in_ref[:width].T, w_in_ref[width:].T], axis=0)
    )
    w_top_ref[...] = w_top[units:]
    w_low_ref[...] = w_low[units:]
    normed_t = split(layer_norm(x_t_ref[...], axis=0))
    straight = dot_halves((w_top, w_low), normed_t)
    kind = faces_ref[1:2, :]
    receiver = faces_ref[0:1, :].astype(F32).astype(BF)
    source = faces_ref[2:3, :].astype(F32)
    cells = jnp.where(kind == 0, source, -1.0).astype(BF)
    halo_rows = jnp.where(kind == 0, -1.0, jnp.where(kind == 1, source, source + halos))
    halo_rows = halo_rows.astype(BF)
    live = lax.broadcasted_iota(I32, (1, slots), 1) < live_ref[...]
    top, low = split(jnp.where(live, weight_ref[...], 0.0))
    out_of = jnp.concatenate(
        [
            small_chosen(cells, rows, top), small_chosen(halo_rows, 2 * halos, top),
            small_chosen(cells, rows, low), small_chosen(halo_rows, 2 * halos, low),
        ],
        axis=0,
    )
    both = dot_bf(out_of, small_chosen(receiver, rows, jnp.ones_like(receiver)), NT)
    sources = rows + 2 * halos
    matrix_t = both[:sources] + both[sources:]
    halo_mat_ref[...] = matrix_t[rows:]
    pre_t_ref[...] = straight[:units] + dot(straight[units:], matrix_t[:rows])


def every_index(head_ref, own_ref, other_ref):
    own = own_ref.shape[1]
    if other_ref.shape[1] > own:
        return other_ref[...]
    first = head_ref[0] == 0
    return jnp.concatenate(
        [
            jnp.where(first, own_ref[...], other_ref[...]),
            jnp.where(first, other_ref[...], own_ref[...]),
        ],
        axis=1,
    )


def hidden_kernel(
    head_ref, own_ref, other_ref, lower_ref, upper_ref, pre_t_ref, halo_mat_ref, w_top_ref,
    w_low_ref, w_out_t_ref, top_ref, low_ref, anchor_ref,
):
    halo_t = jnp.concatenate([lower_ref[...], upper_ref[...]], axis=0).T
    halo_agg = dot(halo_t, halo_mat_ref[...])
    pre = pre_t_ref[...] + dot_halves((w_top_ref[...], w_low_ref[...]), split(halo_agg))
    units, rows = pre.shape
    halves = split(0.5 * pre * (1.0 + lax.erf(pre * math.sqrt(0.5))))
    pick = chosen(every_index(head_ref, own_ref, other_ref), rows)
    anchors = dot_bf(jnp.concatenate(halves, axis=0), pick).astype(BF)
    part = dot_halves(split(w_out_t_ref[...]), (anchors[:units], anchors[units:]))
    anchor_ref[...] = part.T
    top_ref[...], low_ref[...] = halves


def pairs_right(value):
    top, low = split(value)
    return jnp.concatenate([top, top, low, low], axis=1)


def wide(value):
    return jnp.concatenate(split(value), axis=1)


def by_head(value, build):
    return jnp.concatenate(
        [build(value[:, h * DH : (h + 1) * DH]) for h in range(HEADS)], axis=1
    )


def pairs(value_t):
    out = []
    for h in range(HEADS):
        out += split(value_t[h * DH : (h + 1) * DH]) * 2
    return jnp.concatenate(out, axis=0)


def twice(value_t):
    out = []
    for h in range(HEADS):
        out += [value_t[h * DH : (h + 1) * DH]] * 2
    return out


def rest_kernel(
    head_ref, own_ref, other_ref, top_ref, low_ref, w_out_t_ref, x_t_ref, g_t_ref, w_ref,
    wk_ref, wv_ref,
    part_t_ref, anchor_x_ref, d_t_ref, d_pairs_ref, d_wide_ref, k_top_ref, k_low_ref, v_top_ref,
    v_low_ref, back_top_ref, back_low_ref,
):
    part_t_ref[...] = dot_halves(split(w_out_t_ref[...]), (top_ref[...], low_ref[...]))
    pick = chosen(every_index(head_ref, own_ref, other_ref), x_t_ref.shape[1])
    anchor_x_ref[...] = sum(dot_bf(piece, pick) for piece in exact_parts(x_t_ref[...])).T
    d_t = dot(w_ref[...], g_t_ref[...])
    d_t_ref[...] = d_t
    d_pairs_ref[...] = pairs(d_t)
    d_wide_ref[...] = by_head(d_t.T, wide)
    k_top_ref[...], k_low_ref[...] = split(wk_ref[...])
    v_top_ref[...], v_low_ref[...] = split(wv_ref[...])
    back = jnp.concatenate(twice(wk_ref[...].T) + twice(wv_ref[...].T), axis=0)
    back_top_ref[...], back_low_ref[...] = split(back)


def anchor_kernel(x_ref, part_ref, recv_ref, out_ref):
    out_ref[...] = layer_norm(x_ref[...] + (part_ref[...] + recv_ref[...]))


def query_kernel(x_t_ref, part_ref, recv_ref, w_ref, mixed_t_ref, q_pairs_ref, q_wide_ref):
    mixed_t = x_t_ref[...] + (part_ref[...] + recv_ref[...])
    mixed_t_ref[...] = mixed_t
    q_t = dot(w_ref[...].T, layer_norm(mixed_t, axis=0)) * (1.0 / math.sqrt(DH))
    q_pairs_ref[...] = pairs(q_t * LOG2E)
    q_wide_ref[...] = by_head(q_t.T, wide)


def join_kernel(own, _, *refs):
    out = refs[-1]
    blocks = len(refs) - 1
    for place in range(refs[0].shape[0] // own):
        for i, ref in enumerate(refs[:-1]):
            out[pl.ds((place * blocks + i) * own, own), :] = ref[pl.ds(place * own, own), :]


CHUNK = 512


def over_chunks(count, step, carry):
    size = min(count, CHUNK)
    if count == size:
        return step(0, size, carry)
    return lax.fori_loop(
        0, count // size, lambda i, c: step(pl.multiple_of(i * size, size), size, c), carry
    )


def of_head(h, wide_by):
    return slice(wide_by * h * DH, wide_by * (h + 1) * DH)


def score(head_ref, feat_ref, q_pairs_ref, d_pairs_ref, wk, wv, s_ref, dp_ref, v_ref):
    rows = q_pairs_ref.shape[1]
    mine = dp_ref.shape[0]

    def step(start, size, carry):
        at = pl.ds(start, size)
        feat = split(feat_ref[at, :])
        k = dot_halves(feat, wk)
        v = dot_halves(feat, wv)
        v_ref[at, :] = by_head(v, wide)
        for h in range(HEADS):
            s_ref[at, h * rows : (h + 1) * rows] = dot_bf(
                pairs_right(k[:, of_head(h, 1)]), q_pairs_ref[of_head(h, 4), :]
            )
        return carry

    over_chunks(feat_ref.shape[0], step, 0)
    place = pl.ds(pl.multiple_of(head_ref[0] * mine, mine), mine)
    for h in range(HEADS):
        v = v_ref[place, of_head(h, 2)]
        top, low = v[:, :DH], v[:, DH:]
        v_pairs = jnp.concatenate([top, top, low, low], axis=1)
        dp_ref[:, h * rows : (h + 1) * rows] = dot_bf(v_pairs, d_pairs_ref[of_head(h, 4), :])


def score_kernel(
    head_ref, feat_ref, q_pairs_ref, d_pairs_ref, k_top_ref, k_low_ref, v_top_ref, v_low_ref,
    s_ref, dp_ref, v_ref,
):
    wk, wv = (k_top_ref[...], k_low_ref[...]), (v_top_ref[...], v_low_ref[...])
    score(head_ref, feat_ref, q_pairs_ref, d_pairs_ref, wk, wv, s_ref, dp_ref, v_ref)


def attention_kernel(
    head_ref, s_a_ref, dp_a_ref, v_a_ref, feat_ref, q_pairs_ref, q_wide_ref, d_t_ref,
    d_pairs_ref, d_wide_ref, k_top_ref, k_low_ref, v_top_ref, v_low_ref, back_top_ref,
    back_low_ref, att_t_ref, keep_ref, give_ref, s_b_ref, dp_b_ref, v_b_ref,
):
    wk, wv = (k_top_ref[...], k_low_ref[...]), (v_top_ref[...], v_low_ref[...])
    score(head_ref, feat_ref, q_pairs_ref, d_pairs_ref, wk, wv, s_b_ref, dp_b_ref, v_b_ref)
    rows = d_t_ref.shape[1]
    count = feat_ref.shape[0]
    mine = dp_a_ref.shape[0]
    halves = ((s_a_ref, v_a_ref), (s_b_ref, v_b_ref))
    place = pl.ds(pl.multiple_of(head_ref[0] * mine, mine), mine)
    heads = range(HEADS)
    cells = [slice(h * rows, (h + 1) * rows) for h in heads]
    tops, totals, accs = [], [], []
    for h in heads:

        def highest(start, size, top, h=h):
            for s, _ in halves:
                part = jnp.max(s[pl.ds(start, size), cells[h]], axis=0, keepdims=True)
                top = part if top is None else jnp.maximum(top, part)
            return top

        low = None if count <= CHUNK else jnp.full((1, rows), -jnp.inf, F32)
        tops.append(over_chunks(count, highest, low))
    for h in heads:

        def weigh(start, size, state, h=h):
            total, acc = state
            at = pl.ds(start, size)
            for s, v in halves:
                expo = jnp.exp2(s[at, cells[h]] - tops[h])
                top, low = split(expo)
                value = v[at, of_head(h, 2)]
                total = total + jnp.sum(expo, axis=0, keepdims=True)
                acc = acc + (dot_bf(value, top, TN) + dot_bf(value, low, TN))
            return total, acc

        start = (jnp.zeros((1, rows), F32), jnp.zeros((2 * DH, rows), F32))
        total, acc = over_chunks(count, weigh, start)
        totals.append(total)
        accs.append(acc)
    grads_k, grads_v = [], []
    for h in heads:
        inverse = 1.0 / totals[h]
        att = (accs[h][:DH] + accs[h][DH:]) * inverse
        att_t_ref[of_head(h, 1), :] = att
        delta = jnp.sum(d_t_ref[of_head(h, 1), :] * att, axis=0, keepdims=True)
        own = jnp.concatenate([s[place, cells[h]] for s, _ in halves], axis=0)
        d_prob = jnp.concatenate([dp_a_ref[:, cells[h]], dp_b_ref[:, cells[h]]], axis=0)
        probs = jnp.exp2(own - tops[h]) * inverse
        s_top, s_low = split(probs * (d_prob - delta))
        p_top, p_low = split(probs)
        q_wide, d_wide = q_wide_ref[:, of_head(h, 2)], d_wide_ref[:, of_head(h, 2)]
        grads_k.append(dot_bf(s_top, q_wide) + dot_bf(s_low, q_wide))
        grads_v.append(dot_bf(p_top, d_wide) + dot_bf(p_low, d_wide))
    grad = dot_halves(
        split(jnp.concatenate(grads_k + grads_v, axis=1)), (back_top_ref[...], back_low_ref[...])
    )
    keep_ref[...] = grad[:mine]
    give_ref[...] = grad[mine:]


def add_kernel(own, keep_ref, recv_ref, *outs):
    for i, out in enumerate(outs):
        rows = pl.ds(i * own, own)
        out[...] = keep_ref[rows, :] + recv_ref[rows, :]


def output_kernel(mixed_t_ref, att_t_ref, w_ref, out_t_ref):
    out_t_ref[...] = mixed_t_ref[...] + dot(w_ref[...].T, att_t_ref[...])


def sum_kernel(*refs):
    total = refs[0][...]
    for ref in refs[1:-1]:
        total = total + ref[...]
    refs[-1][...] = total


def shards(
    features,
    face_weight,
    faces,
    face_live,
    send_index,
    anchor_index,
    w_in,
    w_out,
    w_query,
    w_key,
    w_value,
    w_attn_out,
    out_grad,
):
    rows, width = features.shape
    halos = send_index.shape[1]
    units = w_in.shape[1]
    own = anchor_index.shape[0]
    n_dom, n_head, n_aux = (lax.axis_size(a) for a in ("dom", "head", "aux"))
    assert n_aux == 2
    anchors = own * n_head
    mine = own * n_dom
    count = anchors * n_dom
    head = lax.axis_index("head").astype(I32).reshape(1)
    swap = [(0, 1), (1, 0)]
    doubling = n_dom & (n_dom - 1) == 0

    def along(value, step):
        return lax.ppermute(value, "dom", [(i, (i + step) % n_dom) for i in range(n_dom)])

    def across(value, step):
        if doubling:
            return lax.ppermute(value, "dom", [(i, i ^ step) for i in range(n_dom)])
        return along(value, step)

    def head_sum(part):
        if n_head == 2:
            return part, lax.ppermute(part, "head", swap)
        return lax.psum(part, "head"), jnp.zeros_like(part)

    x_t, g_t, w_out_t = features.T, out_grad.T, w_out.T
    to_lower, to_upper, index, faces, x_t, w_in = call(
        outgoing_kernel,
        [
            (halos, width), (halos, width), (1, own, I32), (*faces.shape, I32), (width, rows),
            w_in.shape,
        ],
        [send_index, anchor_index.reshape(1, own), faces, x_t, w_in],
        hbm=range(5),
        scratch=[pltpu.VMEM((2, halos), I32), pltpu.SemaphoreType.DMA((5,))],
    )
    from_upper = along(to_lower, n_dom - 1)
    from_lower = along(to_upper, 1)
    if n_head == 2:
        other_index = lax.ppermute(index, "head", swap)
    else:
        other_index = lax.all_gather(index, "head").reshape(1, anchors)
    pre_t, halo_mat, w_top, w_low = call(
        own_faces_kernel,
        [(units, rows), (2 * halos, rows)] + [(units, width, BF)] * 2,
        [face_live.reshape(1, 1), x_t, faces, face_weight.reshape(1, -1), w_in],
        flops=2 * 10**9,
    )
    top, low, anchor_part = call(
        hidden_kernel,
        [(units, rows, BF), (units, rows, BF), (anchors, width)],
        [
            head, index, other_index, from_lower, from_upper, pre_t, halo_mat, w_top, w_low,
            w_out_t,
        ],
        smem=(0,),
        flops=10**9,
    )
    anchor_part, anchor_recv = head_sum(anchor_part)
    part, anchor_x, d_t, d_pairs, d_wide, *weights = call(
        rest_kernel,
        [
            (width, rows), (anchors, width), (width, rows), (4 * width, rows, BF),
            (rows, 2 * width, BF),
        ]
        + [(width, width, BF)] * 4
        + [(4 * width, width, BF)] * 2,
        [
            head, index, other_index, top, low, w_out_t, x_t, g_t, w_attn_out, w_key, w_value,
        ],
        smem=(0,),
        flops=10**9,
    )
    part, recv = head_sum(part)
    (feat,) = call(
        anchor_kernel,
        [(anchors, width)],
        [anchor_x, anchor_part, anchor_recv],
        flops=5 * 10**9,
    )
    feats = [feat] + [across(feat, s) for s in range(1, n_dom)]
    mixed, q_pairs, q_wide = call(
        query_kernel,
        [(width, rows), (4 * width, rows, BF), (rows, 2 * width, BF)],
        [x_t, part, recv, w_query],
        flops=10**9,
    )
    (feat_a,) = call(functools.partial(join_kernel, own), [(count, width)], [mixed] + feats)
    feat_b = lax.ppermute(feat_a, "aux", swap)
    sizes = [(count, HEADS * rows), (mine, HEADS * rows), (count, 2 * width, BF)]
    s_a, dp_a, v_a = call(
        score_kernel,
        sizes,
        [head, feat_a, q_pairs, d_pairs, *weights[:4]],
        smem=(0,),
        flops=10**9,
    )
    att, keep, give = call(
        attention_kernel,
        [(width, rows), (mine, width), (mine, width)],
        [
            head, s_a, dp_a, v_a, feat_b, q_pairs, q_wide, d_t, d_pairs, d_wide, *weights,
        ],
        smem=(0,),
        scratch=[
            pltpu.VMEM(sizes[0], F32), pltpu.VMEM(sizes[1], F32), pltpu.VMEM(sizes[2][:2], BF),
        ],
        flops=2 * 10**9,
    )
    recv = lax.ppermute(give, "aux", swap)
    sums = call(functools.partial(add_kernel, own), [(own, width)] * n_dom, [keep, recv])
    sums = [sums[0]] + [
        across(sums[s], s if doubling else n_dom - s) for s in range(1, n_dom)
    ]
    (output_t,) = call(output_kernel, [(width, rows)], [mixed, att, w_attn_out])
    (anchor_grad,) = call(sum_kernel, [(own, width)], sums)
    return output_t.T, anchor_grad


def solution(mesh):
    placed = (
        P(("groups", "dom", "aux"), None),
        P(("groups", "dom", "aux")),
        P(None, ("groups", "dom", "aux")),
        P(("groups", "dom", "aux")),
        P(None, ("groups", "dom", "aux")),
        P(("groups", "dom", "head", "aux")),
        P(None, "head"),
        P("head", None),
        P(),
        P(),
        P(),
        P(),
        P(("groups", "dom", "aux"), None),
    )
    return jax.shard_map(
        shards,
        mesh=mesh,
        in_specs=placed,
        out_specs=(P(("groups", "dom", "aux"), None), P(("groups", "dom", "head", "aux"), None)),
        check_vma=False,
    )
```

```python
import functools
import math

import jax
import jax.numpy as jnp
from jax import lax
from jax.experimental import pallas as pl
from jax.experimental.pallas import tpu as pltpu
from jax.sharding import PartitionSpec as P

HEADS = 3
DH = 64
NN = (((1,), (0,)), ((), ()))
NT = (((1,), (1,)), ((), ()))
TN = (((0,), (0,)), ((), ()))
BF = jnp.bfloat16
F32 = jnp.float32
I32 = jnp.int32
LOG2E = math.log2(math.e)


def dot_bf(left, right, dims=NN):
    return lax.dot_general(left, right, dims, preferred_element_type=F32)


def split(value):
    top = value.astype(BF)
    return top, (value - top.astype(F32)).astype(BF)


def dot_halves(left, right, dims=NN):
    rows = left[0].shape[0]
    both = dot_bf(jnp.concatenate(left, axis=0), right[0], dims)
    return both[:rows] + (both[rows:] + dot_bf(left[0], right[1], dims))


def dot(left, right, dims=NN):
    return dot_halves(split(left), split(right), dims)


def dense(value):
    rows, width = value.shape
    tail = width % 128
    if tail != 64:
        return value
    tails = jnp.concatenate([value[: rows // 2, -64:], value[rows // 2 :, -64:]], axis=1)
    return jnp.concatenate([value[:, :-64], tails], axis=0)


def undense(value, width):
    if value.shape[1] == width:
        return value
    rows = value.shape[0] * 2 // 3
    tails = jnp.concatenate([value[rows:, :64], value[rows:, 64:]], axis=0)
    return jnp.concatenate([value[:rows], tails], axis=1)


def dense_shape(rows, width):
    return (rows * 3 // 2, 128) if width == 192 else (rows, width)


def layer_norm(value, axis=-1):
    mean = jnp.mean(value, axis=axis, keepdims=True)
    centred = value - mean
    spread = jnp.mean(centred * centred, axis=axis, keepdims=True)
    return centred * lax.rsqrt(spread + 1e-05)


def call(body, outs, ins, smem=(), hbm=(), scratch=(), flops=10**8):
    def space(i):
        return pltpu.SMEM if i in smem else pltpu.HBM if i in hbm else pltpu.VMEM

    return pl.pallas_call(
        body,
        out_shape=[jax.ShapeDtypeStruct(o[:2], o[2] if len(o) > 2 else F32) for o in outs],
        in_specs=[pl.BlockSpec(memory_space=space(i)) for i in range(len(ins))],
        out_specs=[pl.BlockSpec(memory_space=pltpu.VMEM)] * len(outs),
        scratch_shapes=list(scratch),
        compiler_params=pltpu.CompilerParams(vmem_limit_bytes=48 * 2**20),
        cost_estimate=pl.CostEstimate(flops=flops, bytes_accessed=10**6, transcendentals=0),
    )(*[
        pltpu.with_memory_space_constraint(x, pltpu.HBM) if i in hbm else x
        for i, x in enumerate(ins)
    ])


def chosen(index, rows):
    places = lax.broadcasted_iota(I32, (rows, index.shape[1]), 0)
    return jnp.where(places == index, 1.0, 0.0).astype(BF)


def exact_parts(value):
    top, mid = split(value)
    return top, mid, (value - top.astype(F32) - mid.astype(F32)).astype(BF)


def outgoing_kernel(
    send_hbm, index_hbm, faces_hbm, x_t_hbm, w_in_hbm,
    lower_ref, upper_ref, index_ref, faces_ref, x_t_ref, w_in_ref, send_ref, sems,
):
    copies = [
        pltpu.make_async_copy(source, target, sems.at[i])
        for i, (source, target) in enumerate(
            [
                (send_hbm, send_ref), (x_t_hbm, x_t_ref), (index_hbm, index_ref),
                (faces_hbm, faces_ref), (w_in_hbm, w_in_ref),
            ]
        )
    ]
    for copy in copies:
        copy.start()
    copies[0].wait()
    halos = send_ref.shape[1]
    index = jnp.concatenate([send_ref[0:1, :], send_ref[1:2, :]], axis=1)
    pick = chosen(index, x_t_ref.shape[1])
    copies[1].wait()
    top, mid, low = exact_parts(x_t_ref[...])
    sent = layer_norm((dot_bf(top, pick) + dot_bf(mid, pick) + dot_bf(low, pick)).T)
    lower_ref[...] = dense(sent[:halos])
    upper_ref[...] = dense(sent[halos:])
    for copy in copies[2:]:
        copy.wait()


def small_chosen(index, rows, value):
    places = lax.broadcasted_iota(I32, (rows, index.shape[1]), 0).astype(F32).astype(BF)
    return jnp.where(places == index, value, jnp.zeros_like(value))


def own_faces_kernel(
    live_ref, x_t_ref, faces_ref, weight_ref, w_in_ref,
    pre_t_ref, halo_mat_ref, w_top_ref, w_low_ref,
):
    width, rows = x_t_ref.shape
    units = pre_t_ref.shape[0]
    halos = halo_mat_ref.shape[0] // 2
    slots = faces_ref.shape[1]
    w_top, w_low = split(
        jnp.concatenate([w_in_ref[:width].T, w_in_ref[width:].T], axis=0)
    )
    w_top_ref[...] = w_top[units:]
    w_low_ref[...] = w_low[units:]
    normed_t = split(layer_norm(x_t_ref[...], axis=0))
    straight = dot_halves((w_top, w_low), normed_t)
    kind = faces_ref[1:2, :]
    receiver = faces_ref[0:1, :].astype(F32).astype(BF)
    source = faces_ref[2:3, :].astype(F32)
    cells = jnp.where(kind == 0, source, -1.0).astype(BF)
    halo_rows = jnp.where(kind == 0, -1.0, jnp.where(kind == 1, source, source + halos))
    halo_rows = halo_rows.astype(BF)
    live = lax.broadcasted_iota(I32, (1, slots), 1) < live_ref[...]
    top, low = split(jnp.where(live, weight_ref[...], 0.0))
    out_of = jnp.concatenate(
        [
            small_chosen(cells, rows, top), small_chosen(halo_rows, 2 * halos, top),
            small_chosen(cells, rows, low), small_chosen(halo_rows, 2 * halos, low),
        ],
        axis=0,
    )
    both = dot_bf(out_of, small_chosen(receiver, rows, jnp.ones_like(receiver)), NT)
    sources = rows + 2 * halos
    matrix_t = both[:sources] + both[sources:]
    halo_mat_ref[...] = matrix_t[rows:]
    pre_t_ref[...] = straight[:units] + dot(straight[units:], matrix_t[:rows])


def every_index(head_ref, own_ref, other_ref):
    own = own_ref.shape[1]
    if other_ref.shape[1] > own:
        return other_ref[...]
    first = head_ref[0] == 0
    return jnp.concatenate(
        [
            jnp.where(first, own_ref[...], other_ref[...]),
            jnp.where(first, other_ref[...], own_ref[...]),
        ],
        axis=1,
    )


def take(value, pick):
    rows = value.shape[0]
    taken = dot_bf(jnp.concatenate(exact_parts(value), axis=0), pick)
    return taken[:rows] + (taken[rows : 2 * rows] + taken[2 * rows :])


def pick_kernel(
    head_ref, own_ref, other_ref, pre_t_ref, halo_mat_ref, x_t_ref,
    pre_pick_ref, halo_pick_ref, anchor_x_ref,
):
    pick = chosen(every_index(head_ref, own_ref, other_ref), pre_t_ref.shape[1])
    pre_pick_ref[...] = take(pre_t_ref[...], pick)
    halo_pick_ref[...] = take(halo_mat_ref[...], pick)
    anchor_x_ref[...] = take(x_t_ref[...], pick).T


def hidden_part(halo_t, halo_mat, pre_t, w_in_halves, w_out_t):
    halo_agg = dot_halves(halo_t, split(halo_mat))
    pre = pre_t + dot_halves(w_in_halves, split(halo_agg))
    hidden = 0.5 * pre * (1.0 + lax.erf(pre * math.sqrt(0.5)))
    return dot(w_out_t, hidden)


def anchor_part_kernel(
    lower_ref, upper_ref, pre_pick_ref, halo_pick_ref, w_top_ref, w_low_ref, w_out_t_ref,
    part_ref, top_ref, low_ref,
):
    width = w_top_ref.shape[1]
    halo = jnp.concatenate(
        [undense(lower_ref[...], width), undense(upper_ref[...], width)], axis=0
    )
    halo_t = split(halo.T)
    part = hidden_part(
        halo_t, halo_pick_ref[...], pre_pick_ref[...], (w_top_ref[...], w_low_ref[...]),
        w_out_t_ref[...],
    )
    part_ref[...] = dense(part.T)
    top_ref[...], low_ref[...] = halo_t


def rest_kernel(
    top_ref, low_ref, halo_mat_ref, pre_t_ref, w_top_ref, w_low_ref, w_out_t_ref, part_t_ref
):
    part_t_ref[...] = hidden_part(
        (top_ref[...], low_ref[...]), halo_mat_ref[...], pre_t_ref[...],
        (w_top_ref[...], w_low_ref[...]), w_out_t_ref[...],
    )


def split_heads(value_t):
    out = []
    for h in range(HEADS):
        out += split(value_t[h * DH : (h + 1) * DH])
    return jnp.concatenate(out, axis=0)


def through(w, value_t, front_refs, back_refs, back_scale):
    width = w.shape[0]
    w, value_t = split(w), split(value_t)
    for h in range(HEADS):
        at = of_head(h, 1)
        front = dot_halves([half[:, at] for half in w], [half[at] for half in value_t])
        rows = front.shape[1]
        halves = split(front)
        backs = split(front.T * back_scale)
        for i in range(2):
            front_refs[i][h * width : (h + 1) * width, :] = halves[i]
            back_refs[i][h * rows : (h + 1) * rows, :] = backs[i]


def cotangent_kernel(
    g_t_ref, w_ref, wv_ref, _,
    d_t_ref, v_top_ref, v_low_ref, t_top_ref, t_low_ref, t_back_top_ref, t_back_low_ref,
):
    d_t = dot(w_ref[...], g_t_ref[...])
    d_t_ref[...] = d_t
    v_top_ref[...], v_low_ref[...] = split(wv_ref[...].T)
    through(
        wv_ref[...], d_t, (t_top_ref, t_low_ref), (t_back_top_ref, t_back_low_ref), 1.0
    )


def anchor_kernel(x_ref, part_ref, recv_ref, _, *outs):
    part = undense(part_ref[...] + recv_ref[...], x_ref.shape[1])
    feat = dense(layer_norm(x_ref[...] + part))
    for out in outs:
        out[...] = feat


def query_kernel(
    x_t_ref, part_ref, recv_ref, w_ref, wk_ref,
    mixed_t_ref, u_top_ref, u_low_ref, u_back_top_ref, u_back_low_ref,
):
    mixed_t = x_t_ref[...] + (part_ref[...] + recv_ref[...])
    mixed_t_ref[...] = mixed_t
    q_t = dot(w_ref[...].T, layer_norm(mixed_t, axis=0)) * (LOG2E / math.sqrt(DH))
    through(
        wk_ref[...], q_t, (u_top_ref, u_low_ref), (u_back_top_ref, u_back_low_ref), 1.0 / LOG2E
    )


def join_kernel(own, _, *refs):
    out = refs[-1]
    blocks = len(refs) - 1
    for i, ref in enumerate(refs[:-1]):
        value = undense(ref[...], out.shape[1])
        for place in range(value.shape[0] // own):
            out[pl.ds((place * blocks + i) * own, own), :] = value[place * own : (place + 1) * own]


CHUNK = 512


def over_chunks(count, step, carry):
    size = min(count, CHUNK)
    if count == size:
        return step(0, size, carry)
    return lax.fori_loop(
        0, count // size, lambda i, c: step(pl.multiple_of(i * size, size), size, c), carry
    )


def of_head(h, wide_by):
    return slice(wide_by * h * DH, wide_by * (h + 1) * DH)


def forward(head_ref, feat_ref, u, t, wv, s_ref, v_ref, s_mine_ref, dp_ref):
    width = feat_ref.shape[1]
    count = feat_ref.shape[0]
    rows = u[0].shape[1]
    mine = dp_ref.shape[0]
    cells = [slice(h * rows, (h + 1) * rows) for h in range(HEADS)]
    feats = [slice(h * width, (h + 1) * width) for h in range(HEADS)]

    def step(start, size, carry):
        at = pl.ds(start, size)
        feat = split(feat_ref[at, :])
        for h in range(HEADS):
            s_ref[at, cells[h]] = dot_halves(feat, [half[feats[h], :] for half in u])
        v_ref[:, at] = split_heads(dot_halves(wv, split(feat_ref[at, :].T)))
        return carry

    over_chunks(count, step, 0)
    tops, totals, sums = [], [], []
    for h in range(HEADS):

        def highest(start, size, top, h=h):
            part = jnp.max(s_ref[pl.ds(start, size), cells[h]], axis=0, keepdims=True)
            return part if top is None else jnp.maximum(top, part)

        least = None if count <= CHUNK else jnp.full((1, rows), -jnp.inf, F32)
        tops.append(over_chunks(count, highest, least))
    for h in range(HEADS):

        def weigh(start, size, state, h=h):
            total, acc = state
            at = pl.ds(start, size)
            expo = jnp.exp2(s_ref[at, cells[h]] - tops[h])
            top, low = split(expo)
            value = v_ref[of_head(h, 2), at]
            total = total + jnp.sum(expo, axis=0, keepdims=True)
            both = dot_bf(value, top)
            return total, acc + (both[:DH] + (both[DH:] + dot_bf(value[:DH], low)))

        start = (jnp.zeros((1, rows), F32), jnp.zeros((DH, rows), F32))
        total, acc = over_chunks(count, weigh, start)
        totals.append(total)
        sums.append(acc)
    place = pl.ds(pl.multiple_of(head_ref[0] * mine, mine), mine)
    s_mine_ref[...] = s_ref[place, :]
    feat = split(feat_ref[place, :])
    for h in range(HEADS):
        dp_ref[:, cells[h]] = dot_halves(feat, [half[feats[h], :] for half in t])
    return tops, totals, sums


def backward(s_mine_ref, dp_ref, tops, inverses, deltas, u_back, t_back):
    rows = tops[0].shape[1]
    probs, d_scores = [], []
    for h in range(HEADS):
        cells = slice(h * rows, (h + 1) * rows)
        prob = jnp.exp2(s_mine_ref[:, cells] - tops[h]) * inverses[h]
        probs.append(prob)
        d_scores.append(prob * (dp_ref[:, cells] - deltas[h]))
    return dot_halves(split(jnp.concatenate(d_scores, axis=1)), u_back) + dot_halves(
        split(jnp.concatenate(probs, axis=1)), t_back
    )


def halves_of(refs):
    return [ref[...] for ref in refs]


def first_half_kernel(
    head_ref, feat_ref, u_top_ref, u_low_ref, t_top_ref, t_low_ref, v_top_ref, v_low_ref,
    s_mine_ref, dp_ref, sums_ref, state_ref, s_ref, v_ref,
):
    tops, totals, sums = forward(
        head_ref, feat_ref, (u_top_ref, u_low_ref), (t_top_ref, t_low_ref),
        halves_of((v_top_ref, v_low_ref)), s_ref, v_ref, s_mine_ref, dp_ref,
    )
    for h in range(HEADS):
        sums_ref[of_head(h, 1), :] = sums[h]
        state_ref[h : h + 1, :] = tops[h]
        state_ref[HEADS + h : HEADS + h + 1, :] = totals[h]


def second_half_kernel(
    head_ref, sums_ref, state_ref, feat_ref, d_t_ref, u_top_ref, u_low_ref, t_top_ref,
    t_low_ref, v_top_ref, v_low_ref, u_back_top_ref, u_back_low_ref, t_back_top_ref,
    t_back_low_ref, att_t_ref, give_ref, out_state_ref, s_ref, v_ref, s_mine_ref, dp_ref,
):
    tops, totals, sums = forward(
        head_ref, feat_ref, (u_top_ref, u_low_ref), (t_top_ref, t_low_ref),
        halves_of((v_top_ref, v_low_ref)), s_ref, v_ref, s_mine_ref, dp_ref,
    )
    inverses, deltas = [], []
    for h in range(HEADS):
        other_top = state_ref[h : h + 1, :]
        other_total = state_ref[HEADS + h : HEADS + h + 1, :]
        top = jnp.maximum(tops[h], other_top)
        factor, other = jnp.exp2(tops[h] - top), jnp.exp2(other_top - top)
        inverse = 1.0 / (totals[h] * factor + other_total * other)
        att = (sums[h] * factor + sums_ref[of_head(h, 1), :] * other) * inverse
        att_t_ref[of_head(h, 1), :] = att
        tops[h] = top
        inverses.append(inverse)
        deltas.append(jnp.sum(d_t_ref[of_head(h, 1), :] * att, axis=0, keepdims=True))
    for i, row in enumerate(tops + inverses + deltas):
        out_state_ref[i : i + 1, :] = row
    give_ref[...] = backward(
        s_mine_ref, dp_ref, tops, inverses, deltas,
        halves_of((u_back_top_ref, u_back_low_ref)), halves_of((t_back_top_ref, t_back_low_ref)),
    )


def keep_kernel(
    s_mine_ref, dp_ref, state_ref, u_back_top_ref, u_back_low_ref, t_back_top_ref,
    t_back_low_ref, keep_ref,
):
    rows = [state_ref[i : i + 1, :] for i in range(3 * HEADS)]
    keep_ref[...] = backward(
        s_mine_ref, dp_ref, rows[:HEADS], rows[HEADS : 2 * HEADS], rows[2 * HEADS :],
        halves_of((u_back_top_ref, u_back_low_ref)), halves_of((t_back_top_ref, t_back_low_ref)),
    )


def add_kernel(own, keep_ref, recv_ref, *outs):
    for i, out in enumerate(outs):
        rows = pl.ds(i * own, own)
        out[...] = dense(keep_ref[rows, :] + recv_ref[rows, :])


def output_kernel(mixed_t_ref, att_t_ref, w_ref, out_t_ref):
    out_t_ref[...] = mixed_t_ref[...] + dot(w_ref[...].T, att_t_ref[...])


def sum_kernel(*refs):
    total = refs[0][...]
    for ref in refs[1:-1]:
        total = total + ref[...]
    refs[-1][...] = undense(total, refs[-1].shape[1])


def shards(
    features,
    face_weight,
    faces,
    face_live,
    send_index,
    anchor_index,
    w_in,
    w_out,
    w_query,
    w_key,
    w_value,
    w_attn_out,
    out_grad,
):
    rows, width = features.shape
    halos = send_index.shape[1]
    units = w_in.shape[1]
    own = anchor_index.shape[0]
    n_dom, n_head, n_aux = (lax.axis_size(a) for a in ("dom", "head", "aux"))
    assert n_aux == 2
    anchors = own * n_head
    mine = own * n_dom
    count = anchors * n_dom
    head = lax.axis_index("head").astype(I32).reshape(1)
    swap = [(0, 1), (1, 0)]

    def along(value, step):
        return lax.ppermute(value, "dom", [(i, (i + step) % n_dom) for i in range(n_dom)])

    def head_sum(part):
        if n_head == 2:
            return part, lax.ppermute(part, "head", swap)
        return lax.psum(part, "head"), jnp.zeros_like(part)

    x_t, g_t, w_out_t = features.T, out_grad.T, w_out.T
    to_lower, to_upper, index, faces, x_t, w_in = call(
        outgoing_kernel,
        [
            dense_shape(halos, width), dense_shape(halos, width), (1, own, I32), (*faces.shape, I32), (width, rows),
            w_in.shape,
        ],
        [send_index, anchor_index.reshape(1, own), faces, x_t, w_in],
        hbm=range(5),
        scratch=[pltpu.VMEM((2, halos), I32), pltpu.SemaphoreType.DMA((5,))],
    )
    from_upper = along(to_lower, n_dom - 1)
    from_lower = along(to_upper, 1)
    if n_head == 2:
        other_index = lax.ppermute(index, "head", swap)
    else:
        other_index = lax.all_gather(index, "head").reshape(1, anchors)
    pre_t, halo_mat, w_top, w_low = call(
        own_faces_kernel,
        [(units, rows), (2 * halos, rows)] + [(units, width, BF)] * 2,
        [face_live.reshape(1, 1), x_t, faces, face_weight.reshape(1, -1), w_in],
        flops=2 * 10**9,
    )
    pre_pick, halo_pick, anchor_x = call(
        pick_kernel,
        [(units, anchors), (2 * halos, anchors), (anchors, width)],
        [head, index, other_index, pre_t, halo_mat, x_t],
        smem=(0,),
    )
    anchor_part, top, low = call(
        anchor_part_kernel,
        [dense_shape(anchors, width)] + [(width, 2 * halos, BF)] * 2,
        [from_lower, from_upper, pre_pick, halo_pick, w_top, w_low, w_out_t],
        flops=10**9,
    )
    anchor_part, anchor_recv = head_sum(anchor_part)
    (part,) = call(
        rest_kernel,
        [(width, rows)],
        [top, low, halo_mat, pre_t, w_top, w_low, w_out_t],
        flops=10**9,
    )
    front = [(HEADS * width, rows, BF)] * 2
    back = [(HEADS * rows, width, BF)] * 2
    d_t, v_top, v_low, t_top, t_low, *t_back = call(
        cotangent_kernel,
        [(width, rows)] + [(width, width, BF)] * 2 + front + back,
        [g_t, w_attn_out, w_value, top],
        flops=10**9,
    )
    part, recv = head_sum(part)
    feats = call(
        anchor_kernel,
        [dense_shape(anchors, width)] * n_dom,
        [anchor_x, anchor_part, anchor_recv, d_t],
        flops=5 * 10**9,
    )
    feats = [feats[0]] + [along(feats[s], s) for s in range(1, n_dom)]
    mixed, u_top, u_low, *u_back = call(
        query_kernel,
        [(width, rows)] + front + back,
        [x_t, part, recv, w_query, w_key],
        flops=10**9,
    )
    fronts = [u_top, u_low, t_top, t_low, v_top, v_low]
    (feat_a,) = call(functools.partial(join_kernel, own), [(count, width)], [mixed] + feats)
    feat_b = lax.ppermute(feat_a, "aux", swap)
    in_mine = (mine, HEADS * rows)
    work = [pltpu.VMEM((count, HEADS * rows), F32), pltpu.VMEM((2 * width, count), BF)]
    s_mine, dp, sums, state = call(
        first_half_kernel,
        [in_mine, in_mine, (width, rows), (8, rows)],
        [head, feat_a, *fronts],
        smem=(0,),
        scratch=work,
        flops=2 * 10**9,
    )
    att, give, state = call(
        second_half_kernel,
        [(width, rows), (mine, width), (16, rows)],
        [head, sums, state, feat_b, d_t, *fronts, *u_back, *t_back],
        smem=(0,),
        scratch=work + [pltpu.VMEM(in_mine, F32)] * 2,
        flops=2 * 10**9,
    )
    recv = lax.ppermute(give, "aux", swap)
    (keep,) = call(
        keep_kernel,
        [(mine, width)],
        [s_mine, dp, state, *u_back, *t_back],
        flops=10**9,
    )
    sums = call(
        functools.partial(add_kernel, own), [dense_shape(own, width)] * n_dom, [keep, recv]
    )
    sums = [sums[0]] + [along(sums[s], n_dom - s) for s in reversed(range(1, n_dom))]
    (output_t,) = call(output_kernel, [(width, rows)], [mixed, att, w_attn_out])
    (anchor_grad,) = call(sum_kernel, [(own, width)], sums)
    return output_t.T, anchor_grad


def solution(mesh):
    placed = (
        P(("groups", "dom", "aux"), None),
        P(("groups", "dom", "aux")),
        P(None, ("groups", "dom", "aux")),
        P(("groups", "dom", "aux")),
        P(None, ("groups", "dom", "aux")),
        P(("groups", "dom", "head", "aux")),
        P(None, "head"),
        P("head", None),
        P(),
        P(),
        P(),
        P(),
        P(("groups", "dom", "aux"), None),
    )
    return jax.shard_map(
        shards,
        mesh=mesh,
        in_specs=placed,
        out_specs=(P(("groups", "dom", "aux"), None), P(("groups", "dom", "head", "aux"), None)),
        check_vma=False,
    )
```

```python
import functools
import math

import jax
import jax.numpy as jnp
from jax import lax
from jax.experimental import pallas as pl
from jax.experimental.pallas import tpu as pltpu
from jax.sharding import PartitionSpec as P

HEADS = 3
DH = 64
NN = (((1,), (0,)), ((), ()))
NT = (((1,), (1,)), ((), ()))
TN = (((0,), (0,)), ((), ()))
BF = jnp.bfloat16
F32 = jnp.float32
I32 = jnp.int32
LOG2E = math.log2(math.e)


def dot_bf(left, right, dims=NN):
    return lax.dot_general(left, right, dims, preferred_element_type=F32)


def split(value):
    top = value.astype(BF)
    return top, (value - top.astype(F32)).astype(BF)


def dot_halves(left, right, dims=NN):
    rows = left[0].shape[0]
    both = dot_bf(jnp.concatenate(left, axis=0), right[0], dims)
    return both[:rows] + (both[rows:] + dot_bf(left[0], right[1], dims))


def dot(left, right, dims=NN):
    return dot_halves(split(left), split(right), dims)


def dense(value):
    rows, width = value.shape
    tail = width % 128
    if tail != 64:
        return value
    tails = jnp.concatenate([value[: rows // 2, -64:], value[rows // 2 :, -64:]], axis=1)
    return jnp.concatenate([value[:, :-64], tails], axis=0)


def undense(value, width):
    if value.shape[1] == width:
        return value
    rows = value.shape[0] * 2 // 3
    tails = jnp.concatenate([value[rows:, :64], value[rows:, 64:]], axis=0)
    return jnp.concatenate([value[:rows], tails], axis=1)


def dense_shape(rows, width):
    return (rows * 3 // 2, 128) if width == 192 else (rows, width)


def layer_norm(value, axis=-1):
    mean = jnp.mean(value, axis=axis, keepdims=True)
    centred = value - mean
    spread = jnp.mean(centred * centred, axis=axis, keepdims=True)
    return centred * lax.rsqrt(spread + 1e-05)


def call(body, outs, ins, smem=(), hbm=(), scratch=(), flops=10**8):
    def space(i):
        return pltpu.SMEM if i in smem else pltpu.HBM if i in hbm else pltpu.VMEM

    return pl.pallas_call(
        body,
        out_shape=[jax.ShapeDtypeStruct(o[:2], o[2] if len(o) > 2 else F32) for o in outs],
        in_specs=[pl.BlockSpec(memory_space=space(i)) for i in range(len(ins))],
        out_specs=[pl.BlockSpec(memory_space=pltpu.VMEM)] * len(outs),
        scratch_shapes=list(scratch),
        compiler_params=pltpu.CompilerParams(vmem_limit_bytes=48 * 2**20),
        cost_estimate=pl.CostEstimate(flops=flops, bytes_accessed=10**6, transcendentals=0),
    )(*[
        pltpu.with_memory_space_constraint(x, pltpu.HBM) if i in hbm else x
        for i, x in enumerate(ins)
    ])


def chosen(index, rows):
    places = lax.broadcasted_iota(I32, (rows, index.shape[1]), 0)
    return jnp.where(places == index, 1.0, 0.0).astype(BF)


def exact_parts(value):
    top, mid = split(value)
    return top, mid, (value - top.astype(F32) - mid.astype(F32)).astype(BF)


def outgoing_kernel(
    send_hbm, index_hbm, faces_hbm, x_t_hbm, w_in_hbm,
    lower_ref, upper_ref, index_ref, index_out_ref, faces_ref, x_t_ref, w_in_ref, send_ref, sems,
):
    copies = [
        pltpu.make_async_copy(source, target, sems.at[i])
        for i, (source, target) in enumerate(
            [
                (send_hbm, send_ref), (x_t_hbm, x_t_ref), (index_hbm, index_ref),
                (faces_hbm, faces_ref), (w_in_hbm, w_in_ref),
            ]
        )
    ]
    for copy in copies:
        copy.start()
    copies[0].wait()
    halos = send_ref.shape[1]
    index = jnp.concatenate([send_ref[0:1, :], send_ref[1:2, :]], axis=1)
    pick = chosen(index, x_t_ref.shape[1])
    copies[1].wait()
    top, mid, low = exact_parts(x_t_ref[...])
    sent = layer_norm((dot_bf(top, pick) + dot_bf(mid, pick) + dot_bf(low, pick)).T)
    lower_ref[...] = dense(sent[:halos])
    upper_ref[...] = dense(sent[halos:])
    for copy in copies[2:]:
        copy.wait()
    index_out_ref[...] = jnp.zeros_like(index_out_ref)
    index_out_ref[0:1, 0 : index_ref.shape[1]] = index_ref[...]


def small_chosen(index, rows, value):
    places = lax.broadcasted_iota(I32, (rows, index.shape[1]), 0).astype(F32).astype(BF)
    return jnp.where(places == index, value, jnp.zeros_like(value))


def own_faces_kernel(
    live_ref, x_t_ref, faces_ref, weight_ref, w_in_ref,
    pre_t_ref, halo_mat_ref, w_top_ref, w_low_ref,
):
    width, rows = x_t_ref.shape
    units = pre_t_ref.shape[0]
    halos = halo_mat_ref.shape[0] // 2
    slots = faces_ref.shape[1]
    w_top, w_low = split(
        jnp.concatenate([w_in_ref[:width].T, w_in_ref[width:].T], axis=0)
    )
    w_top_ref[...] = w_top[units:]
    w_low_ref[...] = w_low[units:]
    normed_t = split(layer_norm(x_t_ref[...], axis=0))
    straight = dot_halves((w_top, w_low), normed_t)
    kind = faces_ref[1:2, :]
    receiver = faces_ref[0:1, :].astype(F32).astype(BF)
    source = faces_ref[2:3, :].astype(F32)
    cells = jnp.where(kind == 0, source, -1.0).astype(BF)
    halo_rows = jnp.where(kind == 0, -1.0, jnp.where(kind == 1, source, source + halos))
    halo_rows = halo_rows.astype(BF)
    live = lax.broadcasted_iota(I32, (1, slots), 1) < live_ref[...]
    top, low = split(jnp.where(live, weight_ref[...], 0.0))
    out_of = jnp.concatenate(
        [
            small_chosen(cells, rows, top), small_chosen(halo_rows, 2 * halos, top),
            small_chosen(cells, rows, low), small_chosen(halo_rows, 2 * halos, low),
        ],
        axis=0,
    )
    both = dot_bf(out_of, small_chosen(receiver, rows, jnp.ones_like(receiver)), NT)
    sources = rows + 2 * halos
    matrix_t = both[:sources] + both[sources:]
    halo_mat_ref[...] = matrix_t[rows:]
    pre_t_ref[...] = straight[:units] + dot(straight[units:], matrix_t[:rows])


def every_index(head_ref, own_ref, other_ref):
    own = own_ref.shape[1]
    if other_ref.shape[0] == 1:
        return other_ref[...]
    first = head_ref[0] == 0
    other_ref = other_ref.at[0:1, 0:own]
    return jnp.concatenate(
        [
            jnp.where(first, own_ref[...], other_ref[...]),
            jnp.where(first, other_ref[...], own_ref[...]),
        ],
        axis=1,
    )


def hidden_kernel(
    head_ref, lower_ref, upper_ref, own_ref, other_ref, pre_t_ref, halo_mat_ref, w_top_ref,
    w_low_ref, w_out_t_ref, top_ref, low_ref, anchor_ref,
):
    width = w_top_ref.shape[1]
    halo_t = jnp.concatenate(
        [undense(lower_ref[...], width), undense(upper_ref[...], width)], axis=0
    ).T
    halo_agg = dot(halo_t, halo_mat_ref[...])
    pre = pre_t_ref[...] + dot_halves((w_top_ref[...], w_low_ref[...]), split(halo_agg))
    units, rows = pre.shape
    halves = split(0.5 * pre * (1.0 + lax.erf(pre * math.sqrt(0.5))))
    pick = chosen(every_index(head_ref, own_ref, other_ref), rows)
    anchors = dot_bf(jnp.concatenate(halves, axis=0), pick).astype(BF)
    part = dot_halves(split(w_out_t_ref[...]), (anchors[:units], anchors[units:]))
    anchor_ref[...] = dense(part.T)
    top_ref[...], low_ref[...] = halves


def split_heads(value_t):
    out = []
    for h in range(HEADS):
        out += split(value_t[h * DH : (h + 1) * DH])
    return jnp.concatenate(out, axis=0)


def rest_kernel(
    head_ref, own_ref, other_ref, top_ref, low_ref, w_out_t_ref, x_t_ref, part_t_ref,
    anchor_x_ref,
):
    part_t_ref[...] = dot_halves(split(w_out_t_ref[...]), (top_ref[...], low_ref[...]))
    pick = chosen(every_index(head_ref, own_ref, other_ref), x_t_ref.shape[1])
    width = x_t_ref.shape[0]
    taken = dot_bf(jnp.concatenate(exact_parts(x_t_ref[...]), axis=0), pick)
    taken = taken[:width] + (taken[width : 2 * width] + taken[2 * width :])
    anchor_x_ref[...] = taken.T


def through(w, value_t, front_refs, back_refs, back_scale):
    width = w.shape[0]
    w, value_t = split(w), split(value_t)
    for h in range(HEADS):
        at = of_head(h, 1)
        front = dot_halves([half[:, at] for half in w], [half[at] for half in value_t])
        rows = front.shape[1]
        halves = split(front)
        backs = split(front.T * back_scale)
        for i in range(2):
            front_refs[i][h * width : (h + 1) * width, :] = halves[i]
            back_refs[i][h * rows : (h + 1) * rows, :] = backs[i]


def cotangent_kernel(
    g_t_ref, w_ref, wv_ref, _,
    d_t_ref, v_top_ref, v_low_ref, t_top_ref, t_low_ref, t_back_top_ref, t_back_low_ref,
):
    d_t = dot(w_ref[...], g_t_ref[...])
    d_t_ref[...] = d_t
    v_top_ref[...], v_low_ref[...] = split(wv_ref[...].T)
    through(
        wv_ref[...], d_t, (t_top_ref, t_low_ref), (t_back_top_ref, t_back_low_ref), 1.0
    )


def anchor_kernel(x_ref, part_ref, recv_ref, _, *outs):
    part = undense(part_ref[...] + recv_ref[...], x_ref.shape[1])
    feat = dense(layer_norm(x_ref[...] + part))
    for out in outs:
        out[...] = feat


def query_kernel(
    x_t_ref, part_ref, recv_ref, w_ref, wk_ref,
    mixed_t_ref, u_top_ref, u_low_ref, u_back_top_ref, u_back_low_ref,
):
    mixed_t = x_t_ref[...] + (part_ref[...] + recv_ref[...])
    mixed_t_ref[...] = mixed_t
    q_t = dot(w_ref[...].T, layer_norm(mixed_t, axis=0)) * (LOG2E / math.sqrt(DH))
    through(
        wk_ref[...], q_t, (u_top_ref, u_low_ref), (u_back_top_ref, u_back_low_ref), 1.0 / LOG2E
    )


def join_kernel(own, _, *refs):
    out = refs[-1]
    blocks = len(refs) - 1
    for i, ref in enumerate(refs[:-1]):
        value = undense(ref[...], out.shape[1])
        for place in range(value.shape[0] // own):
            out[pl.ds((place * blocks + i) * own, own), :] = value[place * own : (place + 1) * own]


CHUNK = 512


def over_chunks(count, step, carry):
    size = min(count, CHUNK)
    if count == size:
        return step(0, size, carry)
    return lax.fori_loop(
        0, count // size, lambda i, c: step(pl.multiple_of(i * size, size), size, c), carry
    )


def of_head(h, wide_by):
    return slice(wide_by * h * DH, wide_by * (h + 1) * DH)


def forward(head_ref, feat_ref, u, t, wv, s_ref, v_ref, s_mine_ref, dp_ref):
    width = feat_ref.shape[1]
    count = feat_ref.shape[0]
    rows = u[0].shape[1]
    mine = dp_ref.shape[0]
    cells = [slice(h * rows, (h + 1) * rows) for h in range(HEADS)]
    feats = [slice(h * width, (h + 1) * width) for h in range(HEADS)]

    def step(start, size, carry):
        at = pl.ds(start, size)
        feat = split(feat_ref[at, :])
        for h in range(HEADS):
            s_ref[at, cells[h]] = dot_halves(feat, [half[feats[h], :] for half in u])
        v_ref[:, at] = split_heads(dot_halves(wv, split(feat_ref[at, :].T)))
        return carry

    over_chunks(count, step, 0)
    tops, totals, sums = [], [], []
    for h in range(HEADS):

        def highest(start, size, top, h=h):
            part = jnp.max(s_ref[pl.ds(start, size), cells[h]], axis=0, keepdims=True)
            return part if top is None else jnp.maximum(top, part)

        least = None if count <= CHUNK else jnp.full((1, rows), -jnp.inf, F32)
        tops.append(over_chunks(count, highest, least))
    for h in range(HEADS):

        def weigh(start, size, state, h=h):
            total, acc = state
            at = pl.ds(start, size)
            expo = jnp.exp2(s_ref[at, cells[h]] - tops[h])
            top, low = split(expo)
            value = v_ref[of_head(h, 2), at]
            total = total + jnp.sum(expo, axis=0, keepdims=True)
            both = dot_bf(value, top)
            return total, acc + (both[:DH] + (both[DH:] + dot_bf(value[:DH], low)))

        start = (jnp.zeros((1, rows), F32), jnp.zeros((DH, rows), F32))
        total, acc = over_chunks(count, weigh, start)
        totals.append(total)
        sums.append(acc)
    place = pl.ds(pl.multiple_of(head_ref[0] * mine, mine), mine)
    s_mine_ref[...] = s_ref[place, :]
    feat = split(feat_ref[place, :])
    for h in range(HEADS):
        dp_ref[:, cells[h]] = dot_halves(feat, [half[feats[h], :] for half in t])
    return tops, totals, sums


def backward(s_mine_ref, dp_ref, tops, inverses, deltas, u_back, t_back):
    rows = tops[0].shape[1]
    probs, d_scores = [], []
    for h in range(HEADS):
        cells = slice(h * rows, (h + 1) * rows)
        prob = jnp.exp2(s_mine_ref[:, cells] - tops[h]) * inverses[h]
        probs.append(prob)
        d_scores.append(prob * (dp_ref[:, cells] - deltas[h]))
    return dot_halves(split(jnp.concatenate(d_scores, axis=1)), u_back) + dot_halves(
        split(jnp.concatenate(probs, axis=1)), t_back
    )


def halves_of(refs):
    return [ref[...] for ref in refs]


def first_half_kernel(
    head_ref, feat_ref, u_top_ref, u_low_ref, t_top_ref, t_low_ref, v_top_ref, v_low_ref,
    s_mine_ref, dp_ref, sums_ref, state_ref, s_ref, v_ref,
):
    tops, totals, sums = forward(
        head_ref, feat_ref, (u_top_ref, u_low_ref), (t_top_ref, t_low_ref),
        halves_of((v_top_ref, v_low_ref)), s_ref, v_ref, s_mine_ref, dp_ref,
    )
    for h in range(HEADS):
        sums_ref[of_head(h, 1), :] = sums[h]
        state_ref[h : h + 1, :] = tops[h]
        state_ref[HEADS + h : HEADS + h + 1, :] = totals[h]


def second_half_kernel(
    head_ref, sums_ref, state_ref, feat_ref, d_t_ref, u_top_ref, u_low_ref, t_top_ref,
    t_low_ref, v_top_ref, v_low_ref, u_back_top_ref, u_back_low_ref, t_back_top_ref,
    t_back_low_ref, att_t_ref, give_ref, out_state_ref, s_ref, v_ref, s_mine_ref, dp_ref,
):
    tops, totals, sums = forward(
        head_ref, feat_ref, (u_top_ref, u_low_ref), (t_top_ref, t_low_ref),
        halves_of((v_top_ref, v_low_ref)), s_ref, v_ref, s_mine_ref, dp_ref,
    )
    inverses, deltas = [], []
    for h in range(HEADS):
        other_top = state_ref[h : h + 1, :]
        other_total = state_ref[HEADS + h : HEADS + h + 1, :]
        top = jnp.maximum(tops[h], other_top)
        factor, other = jnp.exp2(tops[h] - top), jnp.exp2(other_top - top)
        inverse = 1.0 / (totals[h] * factor + other_total * other)
        att = (sums[h] * factor + sums_ref[of_head(h, 1), :] * other) * inverse
        att_t_ref[of_head(h, 1), :] = att
        tops[h] = top
        inverses.append(inverse)
        deltas.append(jnp.sum(d_t_ref[of_head(h, 1), :] * att, axis=0, keepdims=True))
    for i, row in enumerate(tops + inverses + deltas):
        out_state_ref[i : i + 1, :] = row
    give_ref[...] = backward(
        s_mine_ref, dp_ref, tops, inverses, deltas,
        halves_of((u_back_top_ref, u_back_low_ref)), halves_of((t_back_top_ref, t_back_low_ref)),
    )


def keep_kernel(
    s_mine_ref, dp_ref, state_ref, u_back_top_ref, u_back_low_ref, t_back_top_ref,
    t_back_low_ref, keep_ref,
):
    rows = [state_ref[i : i + 1, :] for i in range(3 * HEADS)]
    keep_ref[...] = backward(
        s_mine_ref, dp_ref, rows[:HEADS], rows[HEADS : 2 * HEADS], rows[2 * HEADS :],
        halves_of((u_back_top_ref, u_back_low_ref)), halves_of((t_back_top_ref, t_back_low_ref)),
    )


def add_kernel(own, keep_ref, recv_ref, *outs):
    for i, out in enumerate(outs):
        rows = pl.ds(i * own, own)
        out[...] = dense(keep_ref[rows, :] + recv_ref[rows, :])


def output_kernel(mixed_t_ref, att_t_ref, w_ref, out_t_ref):
    out_t_ref[...] = mixed_t_ref[...] + dot(w_ref[...].T, att_t_ref[...])


def sum_kernel(*refs):
    total = refs[0][...]
    for ref in refs[1:-1]:
        total = total + ref[...]
    refs[-1][...] = undense(total, refs[-1].shape[1])


def shards(
    features,
    face_weight,
    faces,
    face_live,
    send_index,
    anchor_index,
    w_in,
    w_out,
    w_query,
    w_key,
    w_value,
    w_attn_out,
    out_grad,
):
    rows, width = features.shape
    halos = send_index.shape[1]
    units = w_in.shape[1]
    own = anchor_index.shape[0]
    n_dom, n_head, n_aux = (lax.axis_size(a) for a in ("dom", "head", "aux"))
    assert n_aux == 2
    anchors = own * n_head
    mine = own * n_dom
    count = anchors * n_dom
    head = lax.axis_index("head").astype(I32).reshape(1)
    swap = [(0, 1), (1, 0)]

    def along(value, step):
        return lax.ppermute(value, "dom", [(i, (i + step) % n_dom) for i in range(n_dom)])

    def head_sum(part):
        if n_head == 2:
            return part, lax.ppermute(part, "head", swap)
        return lax.psum(part, "head"), jnp.zeros_like(part)

    x_t, g_t, w_out_t = features.T, out_grad.T, w_out.T
    to_lower, to_upper, index, index_out, faces, x_t, w_in = call(
        outgoing_kernel,
        [
            dense_shape(halos, width), dense_shape(halos, width), (1, own, I32),
            (56, 128, I32), (*faces.shape, I32), (width, rows),
            w_in.shape,
        ],
        [send_index, anchor_index.reshape(1, own), faces, x_t, w_in],
        hbm=range(5),
        scratch=[pltpu.VMEM((2, halos), I32), pltpu.SemaphoreType.DMA((5,))],
    )
    from_upper = along(to_lower, n_dom - 1)
    from_lower = along(to_upper, 1)
    if n_head == 2:
        other_index = lax.ppermute(index_out, "head", swap)
    else:
        other_index = lax.all_gather(index, "head").reshape(1, anchors)
    pre_t, halo_mat, w_top, w_low = call(
        own_faces_kernel,
        [(units, rows), (2 * halos, rows)] + [(units, width, BF)] * 2,
        [face_live.reshape(1, 1), x_t, faces, face_weight.reshape(1, -1), w_in],
        flops=2*10**9,
    )
    top, low, anchor_part = call(
        hidden_kernel,
        [(units, rows, BF), (units, rows, BF), dense_shape(anchors, width)],
        [
            head, from_lower, from_upper, index, other_index, pre_t, halo_mat, w_top, w_low,
            w_out_t,
        ],
        smem=(0,),
        flops=10**9,
    )
    anchor_part, anchor_recv = head_sum(anchor_part)
    part, anchor_x = call(
        rest_kernel,
        [(width, rows), (anchors, width)],
        [head, index, other_index, top, low, w_out_t, x_t],
        smem=(0,),
        flops=10**9,
    )
    front = [(HEADS * width, rows, BF)] * 2
    back = [(HEADS * rows, width, BF)] * 2
    d_t, v_top, v_low, t_top, t_low, *t_back = call(
        cotangent_kernel,
        [(width, rows)] + [(width, width, BF)] * 2 + front + back,
        [g_t, w_attn_out, w_value, top],
        flops=10**9,
    )
    part, recv = head_sum(part)
    feats = call(
        anchor_kernel,
        [dense_shape(anchors, width)] * n_dom,
        [anchor_x, anchor_part, anchor_recv, d_t],
        flops=5 * 10**9,
    )
    feats = [feats[0]] + [along(feats[s], s) for s in range(1, n_dom)]
    mixed, u_top, u_low, *u_back = call(
        query_kernel,
        [(width, rows)] + front + back,
        [x_t, part, recv, w_query, w_key],
        flops=10**9,
    )
    fronts = [u_top, u_low, t_top, t_low, v_top, v_low]
    (feat_a,) = call(functools.partial(join_kernel, own), [(count, width)], [mixed] + feats)
    feat_b = lax.ppermute(feat_a, "aux", swap)
    in_mine = (mine, HEADS * rows)
    work = [pltpu.VMEM((count, HEADS * rows), F32), pltpu.VMEM((2 * width, count), BF)]
    s_mine, dp, sums, state = call(
        first_half_kernel,
        [in_mine, in_mine, (width, rows), (8, rows)],
        [head, feat_a, *fronts],
        smem=(0,),
        scratch=work,
        flops=2 * 10**9,
    )
    att, give, state = call(
        second_half_kernel,
        [(width, rows), (mine, width), (16, rows)],
        [head, sums, state, feat_b, d_t, *fronts, *u_back, *t_back],
        smem=(0,),
        scratch=work + [pltpu.VMEM(in_mine, F32)] * 2,
        flops=2 * 10**9,
    )
    recv = lax.ppermute(give, "aux", swap)
    (keep,) = call(
        keep_kernel,
        [(mine, width)],
        [s_mine, dp, state, *u_back, *t_back],
        flops=10**9,
    )
    sums = call(
        functools.partial(add_kernel, own), [dense_shape(own, width)] * n_dom, [keep, recv]
    )
    sums = [sums[0]] + [along(sums[s], n_dom - s) for s in reversed(range(1, n_dom))]
    (output_t,) = call(output_kernel, [(width, rows)], [mixed, att, w_attn_out])
    (anchor_grad,) = call(sum_kernel, [(own, width)], sums)
    return output_t.T, anchor_grad


def solution(mesh):
    placed = (
        P(("groups", "dom", "aux"), None),
        P(("groups", "dom", "aux")),
        P(None, ("groups", "dom", "aux")),
        P(("groups", "dom", "aux")),
        P(None, ("groups", "dom", "aux")),
        P(("groups", "dom", "head", "aux")),
        P(None, "head"),
        P("head", None),
        P(),
        P(),
        P(),
        P(),
        P(("groups", "dom", "aux"), None),
    )
    return jax.shard_map(
        shards,
        mesh=mesh,
        in_specs=placed,
        out_specs=(P(("groups", "dom", "aux"), None), P(("groups", "dom", "head", "aux"), None)),
        check_vma=False,
    )
```

```python
import functools
import math

import jax
import jax.numpy as jnp
from jax import lax
from jax.experimental import pallas as pl
from jax.experimental.pallas import tpu as pltpu
from jax.sharding import PartitionSpec as P

HEADS = 3
DH = 64
NN = (((1,), (0,)), ((), ()))
NT = (((1,), (1,)), ((), ()))
TN = (((0,), (0,)), ((), ()))
BF = jnp.bfloat16
F32 = jnp.float32
I32 = jnp.int32
LOG2E = math.log2(math.e)


def dot_bf(left, right, dims=NN):
    return lax.dot_general(left, right, dims, preferred_element_type=F32)


def split(value):
    top = value.astype(BF)
    return top, (value - top.astype(F32)).astype(BF)


def dot_halves(left, right, dims=NN):
    rows = left[0].shape[0]
    both = dot_bf(jnp.concatenate(left, axis=0), right[0], dims)
    return both[:rows] + (both[rows:] + dot_bf(left[0], right[1], dims))


def dot(left, right, dims=NN):
    return dot_halves(split(left), split(right), dims)


def dense(value):
    rows, width = value.shape
    tail = width % 128
    if tail != 64:
        return value
    tails = jnp.concatenate([value[: rows // 2, -64:], value[rows // 2 :, -64:]], axis=1)
    return jnp.concatenate([value[:, :-64], tails], axis=0)


def undense(value, width):
    if value.shape[1] == width:
        return value
    rows = value.shape[0] * 2 // 3
    tails = jnp.concatenate([value[rows:, :64], value[rows:, 64:]], axis=0)
    return jnp.concatenate([value[:rows], tails], axis=1)


def side_by_side(value):
    rows, columns = value.shape
    parts = max(128 // columns, 1)
    size = rows // parts
    return jnp.concatenate([value[i * size : (i + 1) * size] for i in range(parts)], axis=1)


def below_each_other(value, columns):
    parts = max(128 // columns, 1)
    return jnp.concatenate(
        [value[:, i * columns : (i + 1) * columns] for i in range(parts)], axis=0
    )


def side_shape(rows, columns):
    parts = max(128 // columns, 1)
    return rows // parts, columns * parts


def dense_shape(rows, width):
    return (rows * 3 // 2, 128) if width == 192 else (rows, width)


def layer_norm(value, axis=-1):
    mean = jnp.mean(value, axis=axis, keepdims=True)
    centred = value - mean
    spread = jnp.mean(centred * centred, axis=axis, keepdims=True)
    return centred * lax.rsqrt(spread + 1e-05)


def call(body, outs, ins, smem=(), hbm=(), scratch=(), flops=10**8):
    def space(i):
        return pltpu.SMEM if i in smem else pltpu.HBM if i in hbm else pltpu.VMEM

    return pl.pallas_call(
        body,
        out_shape=[jax.ShapeDtypeStruct(o[:2], o[2] if len(o) > 2 else F32) for o in outs],
        in_specs=[pl.BlockSpec(memory_space=space(i)) for i in range(len(ins))],
        out_specs=[pl.BlockSpec(memory_space=pltpu.VMEM)] * len(outs),
        scratch_shapes=list(scratch),
        compiler_params=pltpu.CompilerParams(vmem_limit_bytes=48 * 2**20),
        cost_estimate=pl.CostEstimate(flops=flops, bytes_accessed=10**6, transcendentals=0),
    )(*[
        pltpu.with_memory_space_constraint(x, pltpu.HBM) if i in hbm else x
        for i, x in enumerate(ins)
    ])


def chosen(index, rows):
    places = lax.broadcasted_iota(I32, (rows, index.shape[1]), 0)
    return jnp.where(places == index, 1.0, 0.0).astype(BF)


def exact_parts(value):
    top, mid = split(value)
    return top, mid, (value - top.astype(F32) - mid.astype(F32)).astype(BF)


def take(value, pick):
    rows = value.shape[0]
    taken = dot_bf(jnp.concatenate(exact_parts(value), axis=0), pick)
    return taken[:rows] + (taken[rows : 2 * rows] + taken[2 * rows :])


def outgoing_kernel(
    send_hbm, index_hbm, faces_hbm, x_t_hbm, w_in_hbm,
    lower_ref, upper_ref, index_ref, index_out_ref, faces_ref, x_t_ref, w_in_ref, send_ref, sems,
):
    copies = [
        pltpu.make_async_copy(source, target, sems.at[i])
        for i, (source, target) in enumerate(
            [
                (send_hbm, send_ref), (x_t_hbm, x_t_ref), (index_hbm, index_ref),
                (faces_hbm, faces_ref), (w_in_hbm, w_in_ref),
            ]
        )
    ]
    for copy in copies:
        copy.start()
    copies[0].wait()
    halos = send_ref.shape[1]
    index = jnp.concatenate([send_ref[0:1, :], send_ref[1:2, :]], axis=1)
    pick = chosen(index, x_t_ref.shape[1])
    copies[1].wait()
    sent = layer_norm(take(x_t_ref[...], pick), axis=0)
    lower_ref[...] = side_by_side(sent[:, :halos])
    upper_ref[...] = side_by_side(sent[:, halos:])
    for copy in copies[2:]:
        copy.wait()
    index_out_ref[...] = jnp.zeros_like(index_out_ref)
    index_out_ref[0:1, 0 : index_ref.shape[1]] = index_ref[...]


def small_chosen(index, rows, value):
    places = lax.broadcasted_iota(I32, (rows, index.shape[1]), 0).astype(F32).astype(BF)
    return jnp.where(places == index, value, jnp.zeros_like(value))


def own_faces_kernel(
    live_ref, x_t_ref, faces_ref, weight_ref, w_in_ref,
    pre_t_ref, halo_mat_ref, w_top_ref, w_low_ref,
):
    width, rows = x_t_ref.shape
    units = pre_t_ref.shape[0]
    halos = halo_mat_ref.shape[0] // 2
    slots = faces_ref.shape[1]
    w_top, w_low = split(
        jnp.concatenate([w_in_ref[:width].T, w_in_ref[width:].T], axis=0)
    )
    w_top_ref[...] = w_top[units:]
    w_low_ref[...] = w_low[units:]
    normed_t = split(layer_norm(x_t_ref[...], axis=0))
    straight = dot_halves((w_top, w_low), normed_t)
    kind = faces_ref[1:2, :]
    receiver = faces_ref[0:1, :].astype(F32).astype(BF)
    source = faces_ref[2:3, :].astype(F32)
    cells = jnp.where(kind == 0, source, -1.0).astype(BF)
    halo_rows = jnp.where(kind == 0, -1.0, jnp.where(kind == 1, source, source + halos))
    halo_rows = halo_rows.astype(BF)
    live = lax.broadcasted_iota(I32, (1, slots), 1) < live_ref[...]
    top, low = split(jnp.where(live, weight_ref[...], 0.0))
    out_of = jnp.concatenate(
        [
            small_chosen(cells, rows, top), small_chosen(halo_rows, 2 * halos, top),
            small_chosen(cells, rows, low), small_chosen(halo_rows, 2 * halos, low),
        ],
        axis=0,
    )
    both = dot_bf(out_of, small_chosen(receiver, rows, jnp.ones_like(receiver)), NT)
    sources = rows + 2 * halos
    matrix_t = both[:sources] + both[sources:]
    halo_mat_ref[...] = matrix_t[rows:]
    pre_t_ref[...] = straight[:units] + dot(straight[units:], matrix_t[:rows])


def every_index(head_ref, own_ref, other_ref):
    own = own_ref.shape[1]
    if other_ref.shape[0] == 1:
        return other_ref[...]
    first = head_ref[0] == 0
    other_ref = other_ref.at[0:1, 0:own]
    return jnp.concatenate(
        [
            jnp.where(first, own_ref[...], other_ref[...]),
            jnp.where(first, other_ref[...], own_ref[...]),
        ],
        axis=1,
    )


def hidden_kernel(
    head_ref, lower_ref, upper_ref, own_ref, other_ref, pre_t_ref, halo_mat_ref, w_top_ref,
    w_low_ref, w_out_t_ref, top_ref, low_ref, anchor_ref,
):
    halos = halo_mat_ref.shape[0] // 2
    halo_t = jnp.concatenate(
        [below_each_other(lower_ref[...], halos), below_each_other(upper_ref[...], halos)],
        axis=1,
    )
    halo_agg = dot(halo_t, halo_mat_ref[...])
    pre = pre_t_ref[...] + dot_halves((w_top_ref[...], w_low_ref[...]), split(halo_agg))
    units, rows = pre.shape
    halves = split(0.5 * pre * (1.0 + lax.erf(pre * math.sqrt(0.5))))
    pick = chosen(every_index(head_ref, own_ref, other_ref), rows)
    anchors = dot_bf(jnp.concatenate(halves, axis=0), pick).astype(BF)
    part = dot_halves(split(w_out_t_ref[...]), (anchors[:units], anchors[units:]))
    anchor_ref[...] = side_by_side(part)
    top_ref[...], low_ref[...] = halves


def split_heads(value_t):
    out = []
    for h in range(HEADS):
        out += split(value_t[h * DH : (h + 1) * DH])
    return jnp.concatenate(out, axis=0)


def rest_kernel(
    head_ref, own_ref, other_ref, top_ref, low_ref, w_out_t_ref, x_t_ref, part_t_ref,
    anchor_x_ref,
):
    part_t_ref[...] = dot_halves(split(w_out_t_ref[...]), (top_ref[...], low_ref[...]))
    pick = chosen(every_index(head_ref, own_ref, other_ref), x_t_ref.shape[1])
    anchor_x_ref[...] = take(x_t_ref[...], pick)


def through(w, value_t, front_refs, back_refs, back_scale):
    width = w.shape[0]
    w, value_t = split(w), split(value_t)
    for h in range(HEADS):
        at = of_head(h, 1)
        front = dot_halves([half[:, at] for half in w], [half[at] for half in value_t])
        rows = front.shape[1]
        halves = split(front)
        backs = split(front.T * back_scale)
        for i in range(2):
            front_refs[i][:, h * rows : (h + 1) * rows] = halves[i]
            back_refs[i][h * rows : (h + 1) * rows, :] = backs[i]


def cotangent_kernel(
    g_t_ref, w_ref, wv_ref, _,
    d_t_ref, v_top_ref, v_low_ref, t_top_ref, t_low_ref, t_back_top_ref, t_back_low_ref,
):
    d_t = dot(w_ref[...], g_t_ref[...])
    d_t_ref[...] = d_t
    v_top_ref[...], v_low_ref[...] = split(wv_ref[...].T)
    through(
        wv_ref[...], d_t, (t_top_ref, t_low_ref), (t_back_top_ref, t_back_low_ref), 1.0
    )


def anchor_kernel(x_ref, part_ref, recv_ref, _, *outs):
    part = below_each_other(part_ref[...] + recv_ref[...], x_ref.shape[1])
    feat = dense(layer_norm(x_ref[...] + part, axis=0).T)
    for out in outs:
        out[...] = feat


def query_kernel(
    x_t_ref, part_ref, recv_ref, w_ref, wk_ref,
    mixed_t_ref, u_top_ref, u_low_ref, u_back_top_ref, u_back_low_ref,
):
    mixed_t = x_t_ref[...] + (part_ref[...] + recv_ref[...])
    mixed_t_ref[...] = mixed_t
    q_t = dot(w_ref[...].T, layer_norm(mixed_t, axis=0)) * (LOG2E / math.sqrt(DH))
    through(
        wk_ref[...], q_t, (u_top_ref, u_low_ref), (u_back_top_ref, u_back_low_ref), 1.0 / LOG2E
    )


def join_kernel(own, _, *refs):
    out = refs[-1]
    blocks = len(refs) - 1
    for i, ref in enumerate(refs[:-1]):
        value = undense(ref[...], out.shape[1])
        for place in range(value.shape[0] // own):
            out[pl.ds((place * blocks + i) * own, own), :] = value[place * own : (place + 1) * own]


CHUNK = 512


def over_chunks(count, step, carry):
    size = min(count, CHUNK)
    if count == size:
        return step(0, size, carry)
    return lax.fori_loop(
        0, count // size, lambda i, c: step(pl.multiple_of(i * size, size), size, c), carry
    )


def of_head(h, wide_by):
    return slice(wide_by * h * DH, wide_by * (h + 1) * DH)


def forward(head_ref, feat_ref, u, t, wv, s_ref, v_ref, s_mine_ref, dp_ref):
    count = feat_ref.shape[0]
    rows = u[0].shape[1] // HEADS
    mine = dp_ref.shape[0]
    cells = [slice(h * rows, (h + 1) * rows) for h in range(HEADS)]

    def step(start, size, carry):
        at = pl.ds(start, size)
        feat = split(feat_ref[at, :])
        s_ref[at, :] = dot_halves(feat, halves_of(u))
        v_ref[:, at] = split_heads(dot_halves(wv, split(feat_ref[at, :].T)))
        return carry

    over_chunks(count, step, 0)
    place = pl.ds(pl.multiple_of(head_ref[0] * mine, mine), mine)
    dp_ref[...] = dot_halves(split(feat_ref[place, :]), halves_of(t))

    def highest(start, size, top):
        part = jnp.max(s_ref[pl.ds(start, size), :], axis=0, keepdims=True)
        return part if top is None else jnp.maximum(top, part)

    least = None if count <= CHUNK else jnp.full((1, HEADS * rows), -jnp.inf, F32)
    top = over_chunks(count, highest, least)

    def weigh(start, size, state):
        total, sums = state
        at = pl.ds(start, size)
        expo = jnp.exp2(s_ref[at, :] - top)
        high, low = split(expo)
        total = total + jnp.sum(expo, axis=0, keepdims=True)
        added = []
        for h in range(HEADS):
            value = v_ref[of_head(h, 2), at]
            both = dot_bf(value, high[:, cells[h]])
            low_part = dot_bf(value[:DH], low[:, cells[h]])
            added.append(sums[h] + (both[:DH] + (both[DH:] + low_part)))
        return total, tuple(added)

    start = (
        jnp.zeros((1, HEADS * rows), F32),
        tuple(jnp.zeros((DH, rows), F32) for _ in range(HEADS)),
    )
    total, sums = over_chunks(count, weigh, start)
    s_mine_ref[...] = s_ref[place, :]
    return top, total, sums


def backward(s_mine_ref, dp_ref, top, inverse, delta, u_back, t_back):
    probs = jnp.exp2(s_mine_ref[...] - top) * inverse
    d_scores = probs * (dp_ref[...] - delta)
    return dot_halves(split(d_scores), u_back) + dot_halves(split(probs), t_back)


def halves_of(refs):
    return [ref[...] for ref in refs]


def first_half_kernel(
    head_ref, feat_ref, u_top_ref, u_low_ref, t_top_ref, t_low_ref, v_top_ref, v_low_ref,
    s_mine_ref, dp_ref, sums_ref, state_ref, s_ref, v_ref,
):
    top, total, sums = forward(
        head_ref, feat_ref, (u_top_ref, u_low_ref), (t_top_ref, t_low_ref),
        halves_of((v_top_ref, v_low_ref)), s_ref, v_ref, s_mine_ref, dp_ref,
    )
    for h in range(HEADS):
        sums_ref[of_head(h, 1), :] = sums[h]
    state_ref[0:1, :] = top
    state_ref[1:2, :] = total


def second_half_kernel(
    head_ref, sums_ref, state_ref, feat_ref, d_t_ref, u_top_ref, u_low_ref, t_top_ref,
    t_low_ref, v_top_ref, v_low_ref, u_back_top_ref, u_back_low_ref, t_back_top_ref,
    t_back_low_ref, att_t_ref, give_ref, out_state_ref, s_ref, v_ref, s_mine_ref, dp_ref,
):
    top, total, sums = forward(
        head_ref, feat_ref, (u_top_ref, u_low_ref), (t_top_ref, t_low_ref),
        halves_of((v_top_ref, v_low_ref)), s_ref, v_ref, s_mine_ref, dp_ref,
    )
    rows = d_t_ref.shape[1]
    other_top, other_total = state_ref[0:1, :], state_ref[1:2, :]
    new = jnp.maximum(top, other_top)
    factor, other = jnp.exp2(top - new), jnp.exp2(other_top - new)
    inverse = 1.0 / (total * factor + other_total * other)
    deltas = []
    for h in range(HEADS):
        at, cells = of_head(h, 1), slice(h * rows, (h + 1) * rows)
        att = sums[h] * factor[:, cells] + sums_ref[at, :] * other[:, cells]
        att = att * inverse[:, cells]
        att_t_ref[at, :] = att
        deltas.append(jnp.sum(d_t_ref[at, :] * att, axis=0, keepdims=True))
    delta = jnp.concatenate(deltas, axis=1)
    for i, row in enumerate((new, inverse, delta)):
        out_state_ref[i : i + 1, :] = row
    give_ref[...] = backward(
        s_mine_ref, dp_ref, new, inverse, delta,
        halves_of((u_back_top_ref, u_back_low_ref)), halves_of((t_back_top_ref, t_back_low_ref)),
    )


def keep_kernel(
    s_mine_ref, dp_ref, state_ref, u_back_top_ref, u_back_low_ref, t_back_top_ref,
    t_back_low_ref, keep_ref,
):
    keep_ref[...] = backward(
        s_mine_ref, dp_ref, state_ref[0:1, :], state_ref[1:2, :], state_ref[2:3, :],
        halves_of((u_back_top_ref, u_back_low_ref)), halves_of((t_back_top_ref, t_back_low_ref)),
    )


def add_kernel(own, keep_ref, recv_ref, *outs):
    for i, out in enumerate(outs):
        rows = pl.ds(i * own, own)
        out[...] = dense(keep_ref[rows, :] + recv_ref[rows, :])


def output_kernel(mixed_t_ref, att_t_ref, w_ref, out_t_ref):
    out_t_ref[...] = mixed_t_ref[...] + dot(w_ref[...].T, att_t_ref[...])


def sum_kernel(*refs):
    total = refs[0][...]
    for ref in refs[1:-1]:
        total = total + ref[...]
    refs[-1][...] = undense(total, refs[-1].shape[1])


def shards(
    features,
    face_weight,
    faces,
    face_live,
    send_index,
    anchor_index,
    w_in,
    w_out,
    w_query,
    w_key,
    w_value,
    w_attn_out,
    out_grad,
):
    rows, width = features.shape
    halos = send_index.shape[1]
    units = w_in.shape[1]
    own = anchor_index.shape[0]
    n_dom, n_head, n_aux = (lax.axis_size(a) for a in ("dom", "head", "aux"))
    assert n_aux == 2
    anchors = own * n_head
    mine = own * n_dom
    count = anchors * n_dom
    head = lax.axis_index("head").astype(I32).reshape(1)
    swap = [(0, 1), (1, 0)]

    def along(value, step):
        return lax.ppermute(value, "dom", [(i, (i + step) % n_dom) for i in range(n_dom)])

    def head_sum(part):
        if n_head == 2:
            return part, lax.ppermute(part, "head", swap)
        return lax.psum(part, "head"), jnp.zeros_like(part)

    x_t, g_t, w_out_t = features.T, out_grad.T, w_out.T
    to_lower, to_upper, index, index_out, faces, x_t, w_in = call(
        outgoing_kernel,
        [
            side_shape(width, halos), side_shape(width, halos), (1, own, I32),
            (56, 128, I32), (*faces.shape, I32), (width, rows),
            w_in.shape,
        ],
        [send_index, anchor_index.reshape(1, own), faces, x_t, w_in],
        hbm=range(5),
        scratch=[pltpu.VMEM((2, halos), I32), pltpu.SemaphoreType.DMA((5,))],
    )
    from_upper = along(to_lower, n_dom - 1)
    from_lower = along(to_upper, 1)
    if n_head == 2:
        other_index = lax.ppermute(index_out, "head", swap)
    else:
        other_index = lax.all_gather(index, "head").reshape(1, anchors)
    pre_t, halo_mat, w_top, w_low = call(
        own_faces_kernel,
        [(units, rows), (2 * halos, rows)] + [(units, width, BF)] * 2,
        [face_live.reshape(1, 1), x_t, faces, face_weight.reshape(1, -1), w_in],
        flops=2*10**9,
    )
    top, low, anchor_part = call(
        hidden_kernel,
        [(units, rows, BF), (units, rows, BF), side_shape(width, anchors)],
        [
            head, from_lower, from_upper, index, other_index, pre_t, halo_mat, w_top, w_low,
            w_out_t,
        ],
        smem=(0,),
        flops=10**9,
    )
    anchor_part, anchor_recv = head_sum(anchor_part)
    part, anchor_x = call(
        rest_kernel,
        [(width, rows), (width, anchors)],
        [head, index, other_index, top, low, w_out_t, x_t],
        smem=(0,),
        flops=10**9,
    )
    front = [(width, HEADS * rows, BF)] * 2
    back = [(HEADS * rows, width, BF)] * 2
    d_t, v_top, v_low, t_top, t_low, *t_back = call(
        cotangent_kernel,
        [(width, rows)] + [(width, width, BF)] * 2 + front + back,
        [g_t, w_attn_out, w_value, top],
        flops=10**9,
    )
    part, recv = head_sum(part)
    feats = call(
        anchor_kernel,
        [dense_shape(anchors, width)] * n_dom,
        [anchor_x, anchor_part, anchor_recv, d_t],
        flops=5 * 10**9,
    )
    feats = [feats[0]] + [along(feats[s], s) for s in range(1, n_dom)]
    mixed, u_top, u_low, *u_back = call(
        query_kernel,
        [(width, rows)] + front + back,
        [x_t, part, recv, w_query, w_key],
        flops=10**9,
    )
    fronts = [u_top, u_low, t_top, t_low, v_top, v_low]
    (feat_a,) = call(functools.partial(join_kernel, own), [(count, width)], [mixed] + feats)
    feat_b = lax.ppermute(feat_a, "aux", swap)
    in_mine = (mine, HEADS * rows)
    work = [pltpu.VMEM((count, HEADS * rows), F32), pltpu.VMEM((2 * width, count), BF)]
    s_mine, dp, sums, state = call(
        first_half_kernel,
        [in_mine, in_mine, (width, rows), (8, HEADS * rows)],
        [head, feat_a, *fronts],
        smem=(0,),
        scratch=work,
        flops=2 * 10**9,
    )
    att, give, state = call(
        second_half_kernel,
        [(width, rows), (mine, width), (8, HEADS * rows)],
        [head, sums, state, feat_b, d_t, *fronts, *u_back, *t_back],
        smem=(0,),
        scratch=work + [pltpu.VMEM(in_mine, F32)] * 2,
        flops=2 * 10**9,
    )
    recv = lax.ppermute(give, "aux", swap)
    (keep,) = call(
        keep_kernel,
        [(mine, width)],
        [s_mine, dp, state, *u_back, *t_back],
        flops=10**9,
    )
    sums = call(
        functools.partial(add_kernel, own), [dense_shape(own, width)] * n_dom, [keep, recv]
    )
    sums = [sums[0]] + [along(sums[s], n_dom - s) for s in reversed(range(1, n_dom))]
    (output_t,) = call(output_kernel, [(width, rows)], [mixed, att, w_attn_out])
    (anchor_grad,) = call(sum_kernel, [(own, width)], sums)
    return output_t.T, anchor_grad


def solution(mesh):
    placed = (
        P(("groups", "dom", "aux"), None),
        P(("groups", "dom", "aux")),
        P(None, ("groups", "dom", "aux")),
        P(("groups", "dom", "aux")),
        P(None, ("groups", "dom", "aux")),
        P(("groups", "dom", "head", "aux")),
        P(None, "head"),
        P("head", None),
        P(),
        P(),
        P(),
        P(),
        P(("groups", "dom", "aux"), None),
    )
    return jax.shard_map(
        shards,
        mesh=mesh,
        in_specs=placed,
        out_specs=(P(("groups", "dom", "aux"), None), P(("groups", "dom", "head", "aux"), None)),
        check_vma=False,
    )
```

```python
import functools
import math

import jax
import jax.numpy as jnp
from jax import lax
from jax.experimental import pallas as pl
from jax.experimental.pallas import tpu as pltpu
from jax.sharding import PartitionSpec as P

HEADS = 3
DH = 64
NN = (((1,), (0,)), ((), ()))
NT = (((1,), (1,)), ((), ()))
TN = (((0,), (0,)), ((), ()))
BF = jnp.bfloat16
F32 = jnp.float32
I32 = jnp.int32
LOG2E = math.log2(math.e)


def dot_bf(left, right, dims=NN):
    return lax.dot_general(left, right, dims, preferred_element_type=F32)


def split(value):
    top = value.astype(BF)
    return top, (value - top.astype(F32)).astype(BF)


def dot_halves(left, right, dims=NN):
    rows = left[0].shape[0]
    both = dot_bf(jnp.concatenate(left, axis=0), right[0], dims)
    return both[:rows] + (both[rows:] + dot_bf(left[0], right[1], dims))


def dot(left, right, dims=NN):
    return dot_halves(split(left), split(right), dims)


def dense(value):
    rows, width = value.shape
    tail = width % 128
    if tail != 64:
        return value
    tails = jnp.concatenate([value[: rows // 2, -64:], value[rows // 2 :, -64:]], axis=1)
    return jnp.concatenate([value[:, :-64], tails], axis=0)


def undense(value, width):
    if value.shape[1] == width:
        return value
    rows = value.shape[0] * 2 // 3
    tails = jnp.concatenate([value[rows:, :64], value[rows:, 64:]], axis=0)
    return jnp.concatenate([value[:rows], tails], axis=1)


def side_by_side(value):
    rows, columns = value.shape
    parts = max(128 // columns, 1)
    size = rows // parts
    return jnp.concatenate([value[i * size : (i + 1) * size] for i in range(parts)], axis=1)


def below_each_other(value, columns):
    parts = max(128 // columns, 1)
    return jnp.concatenate(
        [value[:, i * columns : (i + 1) * columns] for i in range(parts)], axis=0
    )


def side_shape(rows, columns):
    parts = max(128 // columns, 1)
    return rows // parts, columns * parts


def dense_shape(rows, width):
    return (rows * 3 // 2, 128) if width == 192 else (rows, width)


def layer_norm(value, axis=-1):
    mean = jnp.mean(value, axis=axis, keepdims=True)
    centred = value - mean
    spread = jnp.mean(centred * centred, axis=axis, keepdims=True)
    return centred * lax.rsqrt(spread + 1e-05)


def call(body, outs, ins, smem=(), hbm=(), scratch=(), flops=10**8):
    def space(i):
        return pltpu.SMEM if i in smem else pltpu.HBM if i in hbm else pltpu.VMEM

    return pl.pallas_call(
        body,
        out_shape=[jax.ShapeDtypeStruct(o[:2], o[2] if len(o) > 2 else F32) for o in outs],
        in_specs=[pl.BlockSpec(memory_space=space(i)) for i in range(len(ins))],
        out_specs=[pl.BlockSpec(memory_space=pltpu.VMEM)] * len(outs),
        scratch_shapes=list(scratch),
        compiler_params=pltpu.CompilerParams(vmem_limit_bytes=48 * 2**20),
        cost_estimate=pl.CostEstimate(flops=flops, bytes_accessed=10**6, transcendentals=0),
    )(*[
        pltpu.with_memory_space_constraint(x, pltpu.HBM) if i in hbm else x
        for i, x in enumerate(ins)
    ])


def chosen(index, rows):
    places = lax.broadcasted_iota(I32, (rows, index.shape[1]), 0)
    return jnp.where(places == index, 1.0, 0.0).astype(BF)


def exact_parts(value):
    top, mid = split(value)
    return top, mid, (value - top.astype(F32) - mid.astype(F32)).astype(BF)


def take(value, pick):
    rows = value.shape[0]
    taken = dot_bf(jnp.concatenate(exact_parts(value), axis=0), pick)
    return taken[:rows] + (taken[rows : 2 * rows] + taken[2 * rows :])


def outgoing_kernel(
    send_hbm, index_hbm, faces_hbm, x_t_hbm, w_in_hbm,
    lower_ref, upper_ref, index_ref, index_out_ref, faces_ref, x_t_ref, w_in_ref, send_ref, sems,
):
    copies = [
        pltpu.make_async_copy(source, target, sems.at[i])
        for i, (source, target) in enumerate(
            [
                (send_hbm, send_ref), (x_t_hbm, x_t_ref), (index_hbm, index_ref),
                (faces_hbm, faces_ref), (w_in_hbm, w_in_ref),
            ]
        )
    ]
    for copy in copies:
        copy.start()
    copies[0].wait()
    halos = send_ref.shape[1]
    index = jnp.concatenate([send_ref[0:1, :], send_ref[1:2, :]], axis=1)
    pick = chosen(index, x_t_ref.shape[1])
    copies[1].wait()
    sent = layer_norm(take(x_t_ref[...], pick), axis=0)
    lower_ref[...] = side_by_side(sent[:, :halos])
    upper_ref[...] = side_by_side(sent[:, halos:])
    for copy in copies[2:]:
        copy.wait()
    index_out_ref[...] = jnp.zeros_like(index_out_ref)
    index_out_ref[0:1, 0 : index_ref.shape[1]] = index_ref[...]


def small_chosen(index, rows, value):
    places = lax.broadcasted_iota(I32, (rows, index.shape[1]), 0).astype(F32).astype(BF)
    return jnp.where(places == index, value, jnp.zeros_like(value))


def own_faces_kernel(
    live_ref, x_t_ref, faces_ref, weight_ref, w_in_ref,
    pre_t_ref, halo_mat_ref, w_top_ref, w_low_ref,
):
    width, rows = x_t_ref.shape
    units = pre_t_ref.shape[0]
    halos = halo_mat_ref.shape[0] // 2
    slots = faces_ref.shape[1]
    w_top, w_low = split(
        jnp.concatenate([w_in_ref[:width].T, w_in_ref[width:].T], axis=0)
    )
    w_top_ref[...] = w_top[units:]
    w_low_ref[...] = w_low[units:]
    normed_t = split(layer_norm(x_t_ref[...], axis=0))
    straight = dot_halves((w_top, w_low), normed_t)
    kind = faces_ref[1:2, :]
    receiver = faces_ref[0:1, :].astype(F32).astype(BF)
    source = faces_ref[2:3, :].astype(F32)
    cells = jnp.where(kind == 0, source, -1.0).astype(BF)
    halo_rows = jnp.where(kind == 0, -1.0, jnp.where(kind == 1, source, source + halos))
    halo_rows = halo_rows.astype(BF)
    live = lax.broadcasted_iota(I32, (1, slots), 1) < live_ref[...]
    top, low = split(jnp.where(live, weight_ref[...], 0.0))
    out_of = jnp.concatenate(
        [
            small_chosen(cells, rows, top), small_chosen(halo_rows, 2 * halos, top),
            small_chosen(cells, rows, low), small_chosen(halo_rows, 2 * halos, low),
        ],
        axis=0,
    )
    both = dot_bf(out_of, small_chosen(receiver, rows, jnp.ones_like(receiver)), NT)
    sources = rows + 2 * halos
    matrix_t = both[:sources] + both[sources:]
    halo_mat_ref[...] = matrix_t[rows:]
    pre_t_ref[...] = straight[:units] + dot(straight[units:], matrix_t[:rows])


def every_index(head_ref, own_ref, other_ref):
    own = own_ref.shape[1]
    if other_ref.shape[0] == 1:
        return other_ref[...]
    first = head_ref[0] == 0
    other_ref = other_ref.at[0:1, 0:own]
    return jnp.concatenate(
        [
            jnp.where(first, own_ref[...], other_ref[...]),
            jnp.where(first, other_ref[...], own_ref[...]),
        ],
        axis=1,
    )


def hidden_kernel(
    head_ref, lower_ref, upper_ref, own_ref, other_ref, pre_t_ref, halo_mat_ref, w_top_ref,
    w_low_ref, w_out_t_ref, top_ref, low_ref, anchor_ref,
):
    halos = halo_mat_ref.shape[0] // 2
    halo_t = jnp.concatenate(
        [below_each_other(lower_ref[...], halos), below_each_other(upper_ref[...], halos)],
        axis=1,
    )
    halo_agg = dot(halo_t, halo_mat_ref[...])
    pre = pre_t_ref[...] + dot_halves((w_top_ref[...], w_low_ref[...]), split(halo_agg))
    rows = pre.shape[1]
    halves = split(0.5 * pre * (1.0 + lax.erf(pre * math.sqrt(0.5))))
    pick = chosen(every_index(head_ref, own_ref, other_ref), rows)
    anchors = [dot_bf(half, pick).astype(BF) for half in halves]
    part = dot_halves(split(w_out_t_ref[...]), anchors)
    anchor_ref[...] = side_by_side(part)
    top_ref[...], low_ref[...] = halves


def split_heads(value_t):
    out = []
    for h in range(HEADS):
        out += split(value_t[h * DH : (h + 1) * DH])
    return jnp.concatenate(out, axis=0)


def rest_kernel(
    head_ref, own_ref, other_ref, top_ref, low_ref, w_out_t_ref, x_t_ref, part_t_ref,
    anchor_x_ref,
):
    part_t_ref[...] = dot_halves(split(w_out_t_ref[...]), (top_ref[...], low_ref[...]))
    pick = chosen(every_index(head_ref, own_ref, other_ref), x_t_ref.shape[1])
    anchor_x_ref[...] = take(x_t_ref[...], pick)


def through(w, value_t, front_refs, back_refs, back_scale):
    width = w.shape[0]
    w, value_t = split(w), split(value_t)
    for h in range(HEADS):
        at = of_head(h, 1)
        front = dot_halves([half[:, at] for half in w], [half[at] for half in value_t])
        rows = front.shape[1]
        halves = split(front)
        backs = split(front.T * back_scale)
        for i in range(2):
            front_refs[i][:, h * rows : (h + 1) * rows] = halves[i]
            back_refs[i][h * rows : (h + 1) * rows, :] = backs[i]


def cotangent_kernel(
    g_t_ref, w_ref, wv_ref, _,
    d_t_ref, v_top_ref, v_low_ref, t_top_ref, t_low_ref, t_back_top_ref, t_back_low_ref,
):
    d_t = dot(w_ref[...], g_t_ref[...])
    d_t_ref[...] = d_t
    v_top_ref[...], v_low_ref[...] = split(wv_ref[...].T)
    through(
        wv_ref[...], d_t, (t_top_ref, t_low_ref), (t_back_top_ref, t_back_low_ref), 1.0
    )


def anchor_kernel(x_ref, part_ref, recv_ref, _, *outs):
    part = below_each_other(part_ref[...] + recv_ref[...], x_ref.shape[1])
    feat = dense(layer_norm(x_ref[...] + part, axis=0).T)
    for out in outs:
        out[...] = feat


def query_kernel(
    x_t_ref, part_ref, recv_ref, w_ref, wk_ref,
    mixed_t_ref, u_top_ref, u_low_ref, u_back_top_ref, u_back_low_ref,
):
    mixed_t = x_t_ref[...] + (part_ref[...] + recv_ref[...])
    mixed_t_ref[...] = mixed_t
    q_t = dot(w_ref[...].T, layer_norm(mixed_t, axis=0)) * (LOG2E / math.sqrt(DH))
    through(
        wk_ref[...], q_t, (u_top_ref, u_low_ref), (u_back_top_ref, u_back_low_ref), 1.0 / LOG2E
    )


def join_kernel(own, _, *refs):
    out = refs[-1]
    blocks = len(refs) - 1
    for i, ref in enumerate(refs[:-1]):
        value = undense(ref[...], out.shape[1])
        for place in range(value.shape[0] // own):
            out[pl.ds((place * blocks + i) * own, own), :] = value[place * own : (place + 1) * own]


CHUNK = 512


def over_chunks(count, step, carry):
    size = min(count, CHUNK)
    if count == size:
        return step(0, size, carry)
    return lax.fori_loop(
        0, count // size, lambda i, c: step(pl.multiple_of(i * size, size), size, c), carry
    )


def of_head(h, wide_by):
    return slice(wide_by * h * DH, wide_by * (h + 1) * DH)


def forward(head_ref, feat_ref, u, t, wv, s_ref, v_ref, s_mine_ref, dp_ref):
    count = feat_ref.shape[0]
    rows = u[0].shape[1] // HEADS
    mine = dp_ref.shape[0]
    cells = [slice(h * rows, (h + 1) * rows) for h in range(HEADS)]

    def step(start, size, carry):
        at = pl.ds(start, size)
        feat = split(feat_ref[at, :])
        s_ref[at, :] = dot_halves(feat, halves_of(u))
        v_ref[:, at] = split_heads(dot_halves(wv, split(feat_ref[at, :].T)))
        return carry

    over_chunks(count, step, 0)
    place = pl.ds(pl.multiple_of(head_ref[0] * mine, mine), mine)
    dp_ref[...] = dot_halves(split(feat_ref[place, :]), halves_of(t))

    def highest(start, size, top):
        part = jnp.max(s_ref[pl.ds(start, size), :], axis=0, keepdims=True)
        return part if top is None else jnp.maximum(top, part)

    least = None if count <= CHUNK else jnp.full((1, HEADS * rows), -jnp.inf, F32)
    top = over_chunks(count, highest, least)

    def weigh(start, size, state):
        total, sums = state
        at = pl.ds(start, size)
        expo = jnp.exp2(s_ref[at, :] - top)
        high, low = split(expo)
        total = total + jnp.sum(expo, axis=0, keepdims=True)
        added = []
        for h in range(HEADS):
            value = v_ref[of_head(h, 2), at]
            both = dot_bf(value, high[:, cells[h]])
            low_part = dot_bf(value[:DH], low[:, cells[h]])
            added.append(sums[h] + (both[:DH] + (both[DH:] + low_part)))
        return total, tuple(added)

    start = (
        jnp.zeros((1, HEADS * rows), F32),
        tuple(jnp.zeros((DH, rows), F32) for _ in range(HEADS)),
    )
    total, sums = over_chunks(count, weigh, start)
    s_mine_ref[...] = s_ref[place, :]
    return top, total, sums


def backward(s_mine_ref, dp_ref, top, inverse, delta, u_back, t_back):
    probs = jnp.exp2(s_mine_ref[...] - top) * inverse
    d_scores = probs * (dp_ref[...] - delta)
    return dot_halves(split(d_scores), u_back) + dot_halves(split(probs), t_back)


def put_blocks(own, value, out):
    size = dense_shape(own, value.shape[1])[0]
    for i in range(value.shape[0] // own):
        out[i * size : (i + 1) * size, :] = dense(value[i * own : (i + 1) * own])


def halves_of(refs):
    return [ref[...] for ref in refs]


def first_half_kernel(
    head_ref, feat_ref, u_top_ref, u_low_ref, t_top_ref, t_low_ref, v_top_ref, v_low_ref,
    s_mine_ref, dp_ref, sums_ref, state_ref, s_ref, v_ref,
):
    top, total, sums = forward(
        head_ref, feat_ref, (u_top_ref, u_low_ref), (t_top_ref, t_low_ref),
        halves_of((v_top_ref, v_low_ref)), s_ref, v_ref, s_mine_ref, dp_ref,
    )
    for h in range(HEADS):
        sums_ref[of_head(h, 1), :] = sums[h]
    state_ref[0:1, :] = top
    state_ref[1:2, :] = total


def second_half_kernel(
    own, head_ref, sums_ref, state_ref, feat_ref, d_t_ref, u_top_ref, u_low_ref, t_top_ref,
    t_low_ref, v_top_ref, v_low_ref, u_back_top_ref, u_back_low_ref, t_back_top_ref,
    t_back_low_ref, att_t_ref, give_ref, out_state_ref, s_ref, v_ref, s_mine_ref, dp_ref,
):
    top, total, sums = forward(
        head_ref, feat_ref, (u_top_ref, u_low_ref), (t_top_ref, t_low_ref),
        halves_of((v_top_ref, v_low_ref)), s_ref, v_ref, s_mine_ref, dp_ref,
    )
    rows = d_t_ref.shape[1]
    other_top, other_total = state_ref[0:1, :], state_ref[1:2, :]
    new = jnp.maximum(top, other_top)
    factor, other = jnp.exp2(top - new), jnp.exp2(other_top - new)
    inverse = 1.0 / (total * factor + other_total * other)
    deltas = []
    for h in range(HEADS):
        at, cells = of_head(h, 1), slice(h * rows, (h + 1) * rows)
        att = sums[h] * factor[:, cells] + sums_ref[at, :] * other[:, cells]
        att = att * inverse[:, cells]
        att_t_ref[at, :] = att
        deltas.append(jnp.sum(d_t_ref[at, :] * att, axis=0, keepdims=True))
    delta = jnp.concatenate(deltas, axis=1)
    for i, row in enumerate((new, inverse, delta)):
        out_state_ref[i : i + 1, :] = row
    grad = backward(
        s_mine_ref, dp_ref, new, inverse, delta,
        halves_of((u_back_top_ref, u_back_low_ref)), halves_of((t_back_top_ref, t_back_low_ref)),
    )
    put_blocks(own, grad, give_ref)


def keep_kernel(
    own, s_mine_ref, dp_ref, state_ref, u_back_top_ref, u_back_low_ref, t_back_top_ref,
    t_back_low_ref, keep_ref,
):
    grad = backward(
        s_mine_ref, dp_ref, state_ref[0:1, :], state_ref[1:2, :], state_ref[2:3, :],
        halves_of((u_back_top_ref, u_back_low_ref)), halves_of((t_back_top_ref, t_back_low_ref)),
    )
    put_blocks(own, grad, keep_ref)


def add_kernel(keep_ref, recv_ref, *outs):
    for i, out in enumerate(outs):
        rows = pl.ds(i * out.shape[0], out.shape[0])
        out[...] = keep_ref[rows, :] + recv_ref[rows, :]


def output_kernel(mixed_t_ref, att_t_ref, w_ref, out_t_ref):
    out_t_ref[...] = mixed_t_ref[...] + dot(w_ref[...].T, att_t_ref[...])


def sum_kernel(*refs):
    total = refs[0][...]
    for ref in refs[1:-1]:
        total = total + ref[...]
    refs[-1][...] = undense(total, refs[-1].shape[1])


def shards(
    features,
    face_weight,
    faces,
    face_live,
    send_index,
    anchor_index,
    w_in,
    w_out,
    w_query,
    w_key,
    w_value,
    w_attn_out,
    out_grad,
):
    rows, width = features.shape
    halos = send_index.shape[1]
    units = w_in.shape[1]
    own = anchor_index.shape[0]
    n_dom, n_head, n_aux = (lax.axis_size(a) for a in ("dom", "head", "aux"))
    assert n_aux == 2
    anchors = own * n_head
    mine = own * n_dom
    count = anchors * n_dom
    head = lax.axis_index("head").astype(I32).reshape(1)
    swap = [(0, 1), (1, 0)]

    def along(value, step):
        return lax.ppermute(value, "dom", [(i, (i + step) % n_dom) for i in range(n_dom)])

    def head_sum(part):
        if n_head == 2:
            return part, lax.ppermute(part, "head", swap)
        return lax.psum(part, "head"), jnp.zeros_like(part)

    x_t, g_t, w_out_t = features.T, out_grad.T, w_out.T
    to_lower, to_upper, index, index_out, faces, x_t, w_in = call(
        outgoing_kernel,
        [
            side_shape(width, halos), side_shape(width, halos), (1, own, I32),
            (56, 128, I32), (*faces.shape, I32), (width, rows),
            w_in.shape,
        ],
        [send_index, anchor_index.reshape(1, own), faces, x_t, w_in],
        hbm=range(5),
        scratch=[pltpu.VMEM((2, halos), I32), pltpu.SemaphoreType.DMA((5,))],
    )
    from_upper = along(to_lower, n_dom - 1)
    from_lower = along(to_upper, 1)
    if n_head == 2:
        other_index = lax.ppermute(index_out, "head", swap)
    else:
        other_index = lax.all_gather(index, "head").reshape(1, anchors)
    pre_t, halo_mat, w_top, w_low = call(
        own_faces_kernel,
        [(units, rows), (2 * halos, rows)] + [(units, width, BF)] * 2,
        [face_live.reshape(1, 1), x_t, faces, face_weight.reshape(1, -1), w_in],
        flops=2*10**9,
    )
    top, low, anchor_part = call(
        hidden_kernel,
        [(units, rows, BF), (units, rows, BF), side_shape(width, anchors)],
        [
            head, from_lower, from_upper, index, other_index, pre_t, halo_mat, w_top, w_low,
            w_out_t,
        ],
        smem=(0,),
        flops=10**9,
    )
    anchor_part, anchor_recv = head_sum(anchor_part)
    part, anchor_x = call(
        rest_kernel,
        [(width, rows), (width, anchors)],
        [head, index, other_index, top, low, w_out_t, x_t],
        smem=(0,),
        flops=10**9,
    )
    front = [(width, HEADS * rows, BF)] * 2
    back = [(HEADS * rows, width, BF)] * 2
    d_t, v_top, v_low, t_top, t_low, *t_back = call(
        cotangent_kernel,
        [(width, rows)] + [(width, width, BF)] * 2 + front + back,
        [g_t, w_attn_out, w_value, top],
        flops=10**9,
    )
    part, recv = head_sum(part)
    feats = call(
        anchor_kernel,
        [dense_shape(anchors, width)] * n_dom,
        [anchor_x, anchor_part, anchor_recv, d_t],
        flops=5 * 10**9,
    )
    feats = [feats[0]] + [along(feats[s], s) for s in range(1, n_dom)]
    mixed, u_top, u_low, *u_back = call(
        query_kernel,
        [(width, rows)] + front + back,
        [x_t, part, recv, w_query, w_key],
        flops=10**9,
    )
    fronts = [u_top, u_low, t_top, t_low, v_top, v_low]
    (feat_a,) = call(functools.partial(join_kernel, own), [(count, width)], [mixed] + feats)
    feat_b = lax.ppermute(feat_a, "aux", swap)
    in_mine = (mine, HEADS * rows)
    work = [pltpu.VMEM((count, HEADS * rows), F32), pltpu.VMEM((2 * width, count), BF)]
    s_mine, dp, sums, state = call(
        first_half_kernel,
        [in_mine, in_mine, (width, rows), (8, HEADS * rows)],
        [head, feat_a, *fronts],
        smem=(0,),
        scratch=work,
        flops=2 * 10**9,
    )
    att, give, state = call(
        functools.partial(second_half_kernel, own),
        [(width, rows), dense_shape(mine, width), (8, HEADS * rows)],
        [head, sums, state, feat_b, d_t, *fronts, *u_back, *t_back],
        smem=(0,),
        scratch=work + [pltpu.VMEM(in_mine, F32)] * 2,
        flops=2 * 10**9,
    )
    recv = lax.ppermute(give, "aux", swap)
    (keep,) = call(
        functools.partial(keep_kernel, own),
        [dense_shape(mine, width)],
        [s_mine, dp, state, *u_back, *t_back],
        flops=10**9,
    )
    sums = call(
        add_kernel, [dense_shape(own, width)] * n_dom, [keep, recv]
    )
    sums = [sums[0]] + [along(sums[s], n_dom - s) for s in reversed(range(1, n_dom))]
    (output_t,) = call(output_kernel, [(width, rows)], [mixed, att, w_attn_out])
    (anchor_grad,) = call(sum_kernel, [(own, width)], sums)
    return output_t.T, anchor_grad


def solution(mesh):
    placed = (
        P(("groups", "dom", "aux"), None),
        P(("groups", "dom", "aux")),
        P(None, ("groups", "dom", "aux")),
        P(("groups", "dom", "aux")),
        P(None, ("groups", "dom", "aux")),
        P(("groups", "dom", "head", "aux")),
        P(None, "head"),
        P("head", None),
        P(),
        P(),
        P(),
        P(),
        P(("groups", "dom", "aux"), None),
    )
    return jax.shard_map(
        shards,
        mesh=mesh,
        in_specs=placed,
        out_specs=(P(("groups", "dom", "aux"), None), P(("groups", "dom", "head", "aux"), None)),
        check_vma=False,
    )
```

```python
import functools
import math

import jax
import jax.numpy as jnp
from jax import lax
from jax.experimental import pallas as pl
from jax.experimental.pallas import tpu as pltpu
from jax.sharding import PartitionSpec as P

HEADS = 3
DH = 64
NN = (((1,), (0,)), ((), ()))
NT = (((1,), (1,)), ((), ()))
TN = (((0,), (0,)), ((), ()))
BF = jnp.bfloat16
F32 = jnp.float32
I32 = jnp.int32
LOG2E = math.log2(math.e)


def dot_bf(left, right, dims=NN):
    return lax.dot_general(left, right, dims, preferred_element_type=F32)


def split(value):
    top = value.astype(BF)
    return top, (value - top.astype(F32)).astype(BF)


def dot_halves(left, right, dims=NN):
    rows = left[0].shape[0]
    both = dot_bf(jnp.concatenate(left, axis=0), right[0], dims)
    return both[:rows] + (both[rows:] + dot_bf(left[0], right[1], dims))


def dot(left, right, dims=NN):
    return dot_halves(split(left), split(right), dims)


def dense(value):
    rows, width = value.shape
    tail = width % 128
    if tail != 64:
        return value
    tails = jnp.concatenate([value[: rows // 2, -64:], value[rows // 2 :, -64:]], axis=1)
    return jnp.concatenate([value[:, :-64], tails], axis=0)


def undense(value, width):
    if value.shape[1] == width:
        return value
    rows = value.shape[0] * 2 // 3
    tails = jnp.concatenate([value[rows:, :64], value[rows:, 64:]], axis=0)
    return jnp.concatenate([value[:rows], tails], axis=1)


def side_by_side(value):
    rows, columns = value.shape
    parts = max(128 // columns, 1)
    size = rows // parts
    return jnp.concatenate([value[i * size : (i + 1) * size] for i in range(parts)], axis=1)


def below_each_other(value, columns):
    parts = max(128 // columns, 1)
    return jnp.concatenate(
        [value[:, i * columns : (i + 1) * columns] for i in range(parts)], axis=0
    )


def side_shape(rows, columns):
    parts = max(128 // columns, 1)
    return rows // parts, columns * parts


def dense_shape(rows, width):
    return (rows * 3 // 2, 128) if width == 192 else (rows, width)


def layer_norm(value, axis=-1):
    mean = jnp.mean(value, axis=axis, keepdims=True)
    centred = value - mean
    spread = jnp.mean(centred * centred, axis=axis, keepdims=True)
    return centred * lax.rsqrt(spread + 1e-05)


def call(body, outs, ins, smem=(), hbm=(), scratch=(), flops=10**8):
    def space(i):
        return pltpu.SMEM if i in smem else pltpu.HBM if i in hbm else pltpu.VMEM

    return pl.pallas_call(
        body,
        out_shape=[jax.ShapeDtypeStruct(o[:2], o[2] if len(o) > 2 else F32) for o in outs],
        in_specs=[pl.BlockSpec(memory_space=space(i)) for i in range(len(ins))],
        out_specs=[pl.BlockSpec(memory_space=pltpu.VMEM)] * len(outs),
        scratch_shapes=list(scratch),
        compiler_params=pltpu.CompilerParams(vmem_limit_bytes=48 * 2**20),
        cost_estimate=pl.CostEstimate(flops=flops, bytes_accessed=10**6, transcendentals=0),
    )(*[
        pltpu.with_memory_space_constraint(x, pltpu.HBM) if i in hbm else x
        for i, x in enumerate(ins)
    ])


def chosen(index, rows):
    places = lax.broadcasted_iota(I32, (rows, index.shape[1]), 0)
    return jnp.where(places == index, 1.0, 0.0).astype(BF)


def exact_parts(value):
    top, mid = split(value)
    return top, mid, (value - top.astype(F32) - mid.astype(F32)).astype(BF)


def take(value, pick):
    rows = value.shape[0]
    taken = dot_bf(jnp.concatenate(exact_parts(value), axis=0), pick)
    return taken[:rows] + (taken[rows : 2 * rows] + taken[2 * rows :])


def outgoing_kernel(
    send_hbm, index_hbm, faces_hbm, x_t_hbm, w_in_hbm,
    lower_ref, upper_ref, index_ref, index_out_ref, faces_ref, x_t_ref, w_in_ref, send_ref, sems,
):
    copies = [
        pltpu.make_async_copy(source, target, sems.at[i])
        for i, (source, target) in enumerate(
            [
                (send_hbm, send_ref), (x_t_hbm, x_t_ref), (index_hbm, index_ref),
                (faces_hbm, faces_ref), (w_in_hbm, w_in_ref),
            ]
        )
    ]
    for copy in copies:
        copy.start()
    copies[0].wait()
    halos = send_ref.shape[1]
    index = jnp.concatenate([send_ref[0:1, :], send_ref[1:2, :]], axis=1)
    pick = chosen(index, x_t_ref.shape[1])
    copies[1].wait()
    sent = layer_norm(take(x_t_ref[...], pick), axis=0)
    lower_ref[...] = side_by_side(sent[:, :halos])
    upper_ref[...] = side_by_side(sent[:, halos:])
    for copy in copies[2:]:
        copy.wait()
    index_out_ref[...] = jnp.zeros_like(index_out_ref)
    index_out_ref[0:1, 0 : index_ref.shape[1]] = index_ref[...]


def small_chosen(index, rows, value):
    places = lax.broadcasted_iota(I32, (rows, index.shape[1]), 0).astype(F32).astype(BF)
    return jnp.where(places == index, value, jnp.zeros_like(value))


def own_faces_kernel(
    live_ref, x_t_ref, faces_ref, weight_ref, w_in_ref,
    pre_t_ref, halo_mat_ref, w_top_ref, w_low_ref,
):
    width, rows = x_t_ref.shape
    units = pre_t_ref.shape[0]
    halos = halo_mat_ref.shape[0] // 2
    slots = faces_ref.shape[1]
    w_top, w_low = split(
        jnp.concatenate([w_in_ref[:width].T, w_in_ref[width:].T], axis=0)
    )
    w_top_ref[...] = w_top[units:]
    w_low_ref[...] = w_low[units:]
    normed_t = split(layer_norm(x_t_ref[...], axis=0))
    straight = dot_halves((w_top, w_low), normed_t)
    kind = faces_ref[1:2, :]
    receiver = faces_ref[0:1, :].astype(F32).astype(BF)
    source = faces_ref[2:3, :].astype(F32)
    cells = jnp.where(kind == 0, source, -1.0).astype(BF)
    halo_rows = jnp.where(kind == 0, -1.0, jnp.where(kind == 1, source, source + halos))
    halo_rows = halo_rows.astype(BF)
    live = lax.broadcasted_iota(I32, (1, slots), 1) < live_ref[...]
    top, low = split(jnp.where(live, weight_ref[...], 0.0))
    out_of = jnp.concatenate(
        [
            small_chosen(cells, rows, top), small_chosen(halo_rows, 2 * halos, top),
            small_chosen(cells, rows, low), small_chosen(halo_rows, 2 * halos, low),
        ],
        axis=0,
    )
    both = dot_bf(out_of, small_chosen(receiver, rows, jnp.ones_like(receiver)), NT)
    sources = rows + 2 * halos
    matrix_t = both[:sources] + both[sources:]
    halo_mat_ref[...] = matrix_t[rows:]
    pre_t_ref[...] = straight[:units] + dot(straight[units:], matrix_t[:rows])


def every_index(head_ref, own_ref, other_ref):
    own = own_ref.shape[1]
    if other_ref.shape[0] == 1:
        return other_ref[...]
    first = head_ref[0] == 0
    other_ref = other_ref.at[0:1, 0:own]
    return jnp.concatenate(
        [
            jnp.where(first, own_ref[...], other_ref[...]),
            jnp.where(first, other_ref[...], own_ref[...]),
        ],
        axis=1,
    )


def hidden_kernel(
    head_ref, lower_ref, upper_ref, own_ref, other_ref, pre_t_ref, halo_mat_ref, w_top_ref,
    w_low_ref, w_out_t_ref, top_ref, low_ref, anchor_ref,
):
    halos = halo_mat_ref.shape[0] // 2
    halo_t = jnp.concatenate(
        [below_each_other(lower_ref[...], halos), below_each_other(upper_ref[...], halos)],
        axis=1,
    )
    halo_agg = dot(halo_t, halo_mat_ref[...])
    pre = pre_t_ref[...] + dot_halves((w_top_ref[...], w_low_ref[...]), split(halo_agg))
    rows = pre.shape[1]
    halves = split(0.5 * pre * (1.0 + lax.erf(pre * math.sqrt(0.5))))
    pick = chosen(every_index(head_ref, own_ref, other_ref), rows)
    anchors = [dot_bf(half, pick).astype(BF) for half in halves]
    part = dot_halves(split(w_out_t_ref[...]), anchors)
    anchor_ref[...] = side_by_side(part)
    top_ref[...], low_ref[...] = halves


def split_heads(value_t):
    out = []
    for h in range(HEADS):
        out += split(value_t[h * DH : (h + 1) * DH])
    return jnp.concatenate(out, axis=0)


def rest_kernel(
    head_ref, own_ref, other_ref, top_ref, low_ref, w_out_t_ref, x_t_ref, part_t_ref,
    anchor_x_ref,
):
    part_t_ref[...] = dot_halves(split(w_out_t_ref[...]), (top_ref[...], low_ref[...]))
    pick = chosen(every_index(head_ref, own_ref, other_ref), x_t_ref.shape[1])
    anchor_x_ref[...] = take(x_t_ref[...], pick)


def through(w, value_t, front_refs, back_refs, back_scale):
    width = w.shape[0]
    w, value_t = split(w), split(value_t)
    for h in range(HEADS):
        at = of_head(h, 1)
        front = dot_halves([half[:, at] for half in w], [half[at] for half in value_t])
        rows = front.shape[1]
        halves = split(front)
        backs = split(front.T * back_scale)
        for i in range(2):
            front_refs[i][:, h * rows : (h + 1) * rows] = halves[i]
            back_refs[i][h * rows : (h + 1) * rows, :] = backs[i]


def cotangent_kernel(
    g_t_ref, w_ref, wv_ref, _,
    d_t_ref, v_top_ref, v_low_ref, t_top_ref, t_low_ref, t_back_top_ref, t_back_low_ref,
):
    d_t = dot(w_ref[...], g_t_ref[...])
    d_t_ref[...] = d_t
    v_top_ref[...], v_low_ref[...] = split(wv_ref[...].T)
    through(
        wv_ref[...], d_t, (t_top_ref, t_low_ref), (t_back_top_ref, t_back_low_ref), 1.0
    )


def anchor_kernel(x_ref, part_ref, recv_ref, _, *outs):
    part = below_each_other(part_ref[...] + recv_ref[...], x_ref.shape[1])
    feat = dense(layer_norm(x_ref[...] + part, axis=0).T)
    for out in outs:
        out[...] = feat


def query_kernel(
    x_t_ref, part_ref, recv_ref, w_ref, wk_ref,
    mixed_t_ref, u_top_ref, u_low_ref, u_back_top_ref, u_back_low_ref,
):
    mixed_t = x_t_ref[...] + (part_ref[...] + recv_ref[...])
    mixed_t_ref[...] = mixed_t
    q_t = dot(w_ref[...].T, layer_norm(mixed_t, axis=0)) * (LOG2E / math.sqrt(DH))
    through(
        wk_ref[...], q_t, (u_top_ref, u_low_ref), (u_back_top_ref, u_back_low_ref), 1.0 / LOG2E
    )


def join_kernel(own, _, *refs):
    out, message = refs[-2:]
    blocks = len(refs) - 2
    for i, ref in enumerate(refs[:-2]):
        value = undense(ref[...], out.shape[1])
        for place in range(value.shape[0] // own):
            out[pl.ds((place * blocks + i) * own, own), :] = value[place * own : (place + 1) * own]
    message[...] = dense(out[...])


CHUNK = 512


def over_chunks(count, step, carry):
    size = min(count, CHUNK)
    if count == size:
        return step(0, size, carry)
    return lax.fori_loop(
        0, count // size, lambda i, c: step(pl.multiple_of(i * size, size), size, c), carry
    )


def of_head(h, wide_by):
    return slice(wide_by * h * DH, wide_by * (h + 1) * DH)


def forward(head_ref, feat_ref, u, t, wv, s_ref, v_ref, s_mine_ref, dp_ref):
    count = feat_ref.shape[0]
    rows = u[0].shape[1] // HEADS
    mine = dp_ref.shape[0]
    cells = [slice(h * rows, (h + 1) * rows) for h in range(HEADS)]

    def step(start, size, carry):
        at = pl.ds(start, size)
        feat = split(feat_ref[at, :])
        s_ref[at, :] = dot_halves(feat, halves_of(u))
        v_ref[:, at] = split_heads(dot_halves(wv, split(feat_ref[at, :].T)))
        return carry

    over_chunks(count, step, 0)
    place = pl.ds(pl.multiple_of(head_ref[0] * mine, mine), mine)
    dp_ref[...] = dot_halves(split(feat_ref[place, :]), halves_of(t))

    def highest(start, size, top):
        part = jnp.max(s_ref[pl.ds(start, size), :], axis=0, keepdims=True)
        return part if top is None else jnp.maximum(top, part)

    least = None if count <= CHUNK else jnp.full((1, HEADS * rows), -jnp.inf, F32)
    top = over_chunks(count, highest, least)

    def weigh(start, size, state):
        total, sums = state
        at = pl.ds(start, size)
        expo = jnp.exp2(s_ref[at, :] - top)
        high, low = split(expo)
        total = total + jnp.sum(expo, axis=0, keepdims=True)
        added = []
        for h in range(HEADS):
            value = v_ref[of_head(h, 2), at]
            both = dot_bf(value, high[:, cells[h]])
            low_part = dot_bf(value[:DH], low[:, cells[h]])
            added.append(sums[h] + (both[:DH] + (both[DH:] + low_part)))
        return total, tuple(added)

    start = (
        jnp.zeros((1, HEADS * rows), F32),
        tuple(jnp.zeros((DH, rows), F32) for _ in range(HEADS)),
    )
    total, sums = over_chunks(count, weigh, start)
    s_mine_ref[...] = s_ref[place, :]
    return top, total, sums


def backward(s_mine_ref, dp_ref, top, inverse, delta, u_back, t_back):
    probs = jnp.exp2(s_mine_ref[...] - top) * inverse
    d_scores = probs * (dp_ref[...] - delta)
    return dot_halves(split(d_scores), u_back) + dot_halves(split(probs), t_back)


def put_blocks(own, value, out):
    size = dense_shape(own, value.shape[1])[0]
    for i in range(value.shape[0] // own):
        out[i * size : (i + 1) * size, :] = dense(value[i * own : (i + 1) * own])


def halves_of(refs):
    return [ref[...] for ref in refs]


def first_half_kernel(
    head_ref, feat_ref, u_top_ref, u_low_ref, t_top_ref, t_low_ref, v_top_ref, v_low_ref,
    s_mine_ref, dp_ref, sums_ref, state_ref, s_ref, v_ref,
):
    top, total, sums = forward(
        head_ref, feat_ref, (u_top_ref, u_low_ref), (t_top_ref, t_low_ref),
        halves_of((v_top_ref, v_low_ref)), s_ref, v_ref, s_mine_ref, dp_ref,
    )
    for h in range(HEADS):
        sums_ref[of_head(h, 1), :] = sums[h]
    state_ref[0:1, :] = top
    state_ref[1:2, :] = total


def second_half_kernel(
    own, head_ref, sums_ref, state_ref, message_ref, d_t_ref, u_top_ref, u_low_ref, t_top_ref,
    t_low_ref, v_top_ref, v_low_ref, u_back_top_ref, u_back_low_ref, t_back_top_ref,
    t_back_low_ref, att_t_ref, give_ref, out_state_ref, s_ref, v_ref, s_mine_ref, dp_ref,
    feat_ref,
):
    feat_ref[...] = undense(message_ref[...], feat_ref.shape[1])
    top, total, sums = forward(
        head_ref, feat_ref, (u_top_ref, u_low_ref), (t_top_ref, t_low_ref),
        halves_of((v_top_ref, v_low_ref)), s_ref, v_ref, s_mine_ref, dp_ref,
    )
    rows = d_t_ref.shape[1]
    other_top, other_total = state_ref[0:1, :], state_ref[1:2, :]
    new = jnp.maximum(top, other_top)
    factor, other = jnp.exp2(top - new), jnp.exp2(other_top - new)
    inverse = 1.0 / (total * factor + other_total * other)
    deltas = []
    for h in range(HEADS):
        at, cells = of_head(h, 1), slice(h * rows, (h + 1) * rows)
        att = sums[h] * factor[:, cells] + sums_ref[at, :] * other[:, cells]
        att = att * inverse[:, cells]
        att_t_ref[at, :] = att
        deltas.append(jnp.sum(d_t_ref[at, :] * att, axis=0, keepdims=True))
    delta = jnp.concatenate(deltas, axis=1)
    for i, row in enumerate((new, inverse, delta)):
        out_state_ref[i : i + 1, :] = row
    grad = backward(
        s_mine_ref, dp_ref, new, inverse, delta,
        halves_of((u_back_top_ref, u_back_low_ref)), halves_of((t_back_top_ref, t_back_low_ref)),
    )
    put_blocks(own, grad, give_ref)


def keep_kernel(
    own, s_mine_ref, dp_ref, state_ref, u_back_top_ref, u_back_low_ref, t_back_top_ref,
    t_back_low_ref, keep_ref,
):
    grad = backward(
        s_mine_ref, dp_ref, state_ref[0:1, :], state_ref[1:2, :], state_ref[2:3, :],
        halves_of((u_back_top_ref, u_back_low_ref)), halves_of((t_back_top_ref, t_back_low_ref)),
    )
    put_blocks(own, grad, keep_ref)


def add_kernel(keep_ref, recv_ref, *outs):
    for i, out in enumerate(outs):
        rows = pl.ds(i * out.shape[0], out.shape[0])
        out[...] = keep_ref[rows, :] + recv_ref[rows, :]


def output_kernel(mixed_t_ref, att_t_ref, w_ref, out_t_ref):
    out_t_ref[...] = mixed_t_ref[...] + dot(w_ref[...].T, att_t_ref[...])


def sum_kernel(*refs):
    total = refs[0][...]
    for ref in refs[1:-1]:
        total = total + ref[...]
    refs[-1][...] = undense(total, refs[-1].shape[1])


def shards(
    features,
    face_weight,
    faces,
    face_live,
    send_index,
    anchor_index,
    w_in,
    w_out,
    w_query,
    w_key,
    w_value,
    w_attn_out,
    out_grad,
):
    rows, width = features.shape
    halos = send_index.shape[1]
    units = w_in.shape[1]
    own = anchor_index.shape[0]
    n_dom, n_head, n_aux = (lax.axis_size(a) for a in ("dom", "head", "aux"))
    assert n_aux == 2
    anchors = own * n_head
    mine = own * n_dom
    count = anchors * n_dom
    head = lax.axis_index("head").astype(I32).reshape(1)
    swap = [(0, 1), (1, 0)]

    def along(value, step):
        return lax.ppermute(value, "dom", [(i, (i + step) % n_dom) for i in range(n_dom)])

    def head_sum(part):
        if n_head == 2:
            return part, lax.ppermute(part, "head", swap)
        return lax.psum(part, "head"), jnp.zeros_like(part)

    x_t, g_t, w_out_t = features.T, out_grad.T, w_out.T
    to_lower, to_upper, index, index_out, faces, x_t, w_in = call(
        outgoing_kernel,
        [
            side_shape(width, halos), side_shape(width, halos), (1, own, I32),
            (56, 128, I32), (*faces.shape, I32), (width, rows),
            w_in.shape,
        ],
        [send_index, anchor_index.reshape(1, own), faces, x_t, w_in],
        hbm=range(5),
        scratch=[pltpu.VMEM((2, halos), I32), pltpu.SemaphoreType.DMA((5,))],
    )
    from_upper = along(to_lower, n_dom - 1)
    from_lower = along(to_upper, 1)
    if n_head == 2:
        other_index = lax.ppermute(index_out, "head", swap)
    else:
        other_index = lax.all_gather(index, "head").reshape(1, anchors)
    pre_t, halo_mat, w_top, w_low = call(
        own_faces_kernel,
        [(units, rows), (2 * halos, rows)] + [(units, width, BF)] * 2,
        [face_live.reshape(1, 1), x_t, faces, face_weight.reshape(1, -1), w_in],
        flops=2*10**9,
    )
    top, low, anchor_part = call(
        hidden_kernel,
        [(units, rows, BF), (units, rows, BF), side_shape(width, anchors)],
        [
            head, from_lower, from_upper, index, other_index, pre_t, halo_mat, w_top, w_low,
            w_out_t,
        ],
        smem=(0,),
        flops=10**9,
    )
    anchor_part, anchor_recv = head_sum(anchor_part)
    part, anchor_x = call(
        rest_kernel,
        [(width, rows), (width, anchors)],
        [head, index, other_index, top, low, w_out_t, x_t],
        smem=(0,),
        flops=10**9,
    )
    front = [(width, HEADS * rows, BF)] * 2
    back = [(HEADS * rows, width, BF)] * 2
    d_t, v_top, v_low, t_top, t_low, *t_back = call(
        cotangent_kernel,
        [(width, rows)] + [(width, width, BF)] * 2 + front + back,
        [g_t, w_attn_out, w_value, top],
        flops=10**9,
    )
    part, recv = head_sum(part)
    feats = call(
        anchor_kernel,
        [dense_shape(anchors, width)] * n_dom,
        [anchor_x, anchor_part, anchor_recv, d_t],
        flops=5 * 10**9,
    )
    feats = [feats[0]] + [along(feats[s], s) for s in range(1, n_dom)]
    mixed, u_top, u_low, *u_back = call(
        query_kernel,
        [(width, rows)] + front + back,
        [x_t, part, recv, w_query, w_key],
        flops=10**9,
    )
    fronts = [u_top, u_low, t_top, t_low, v_top, v_low]
    feat_a, feat_b = call(
        functools.partial(join_kernel, own),
        [(count, width), dense_shape(count, width)],
        [mixed] + feats,
    )
    feat_b = lax.ppermute(feat_b, "aux", swap)
    in_mine = (mine, HEADS * rows)
    work = [pltpu.VMEM((count, HEADS * rows), F32), pltpu.VMEM((2 * width, count), BF)]
    s_mine, dp, sums, state = call(
        first_half_kernel,
        [in_mine, in_mine, (width, rows), (8, HEADS * rows)],
        [head, feat_a, *fronts],
        smem=(0,),
        scratch=work,
        flops=2 * 10**9,
    )
    att, give, state = call(
        functools.partial(second_half_kernel, own),
        [(width, rows), dense_shape(mine, width), (8, HEADS * rows)],
        [head, sums, state, feat_b, d_t, *fronts, *u_back, *t_back],
        smem=(0,),
        scratch=work + [pltpu.VMEM(in_mine, F32)] * 2 + [pltpu.VMEM((count, width), F32)],
        flops=2 * 10**9,
    )
    recv = lax.ppermute(give, "aux", swap)
    (keep,) = call(
        functools.partial(keep_kernel, own),
        [dense_shape(mine, width)],
        [s_mine, dp, state, *u_back, *t_back],
        flops=10**9,
    )
    sums = call(
        add_kernel, [dense_shape(own, width)] * n_dom, [keep, recv]
    )
    sums = [sums[0]] + [along(sums[s], n_dom - s) for s in reversed(range(1, n_dom))]
    (output_t,) = call(output_kernel, [(width, rows)], [mixed, att, w_attn_out])
    (anchor_grad,) = call(sum_kernel, [(own, width)], sums)
    return output_t.T, anchor_grad


def solution(mesh):
    placed = (
        P(("groups", "dom", "aux"), None),
        P(("groups", "dom", "aux")),
        P(None, ("groups", "dom", "aux")),
        P(("groups", "dom", "aux")),
        P(None, ("groups", "dom", "aux")),
        P(("groups", "dom", "head", "aux")),
        P(None, "head"),
        P("head", None),
        P(),
        P(),
        P(),
        P(),
        P(("groups", "dom", "aux"), None),
    )
    return jax.shard_map(
        shards,
        mesh=mesh,
        in_specs=placed,
        out_specs=(P(("groups", "dom", "aux"), None), P(("groups", "dom", "head", "aux"), None)),
        check_vma=False,
    )
```
